256 devices in a mesh: dom: 256 (over y, z, x, core).
Axes of the slice: x: 4, y: 4, z: 8, core: 2. Of those that a mesh axis runs over, the one named last changes fastest.
Arguments:
- node_feats: bfloat16 [8192, 49, 128], P('dom'), may hold values from -6 to 6
- cotangent: bfloat16 [8192, 49, 128], P('dom'), may hold values from -6 to 6
- boundary: int32 [256, 5, 16], P('dom'), may hold values from 0 to 31, as said below
- edge_src: int32 [256, 192], P('dom'), may hold values from 0 to 111
- edge_dst: int32 [256, 192], P('dom'), may hold values from 0 to 31
- edge_dist: float32 [256, 192], P('dom'), may hold values from 0.5 to 4.5
- edge_count: int32 [256], P('dom'), may hold values from 24 to 192, as said below
- w_real: bfloat16 [7, 128, 128], replicated, may hold values from -0.375 to 0.375
- w_imag: bfloat16 [6, 128, 128], replicated, may hold values from -0.375 to 0.375
- w_gate: bfloat16 [128, 8], replicated, may hold values from -0.5 to 0.5
Outputs:
- updated: bfloat16 [8192, 49, 128], P('dom')
- node_grad: float32 [8192, 49, 128], P('dom')
- real_grad: float32 [7, 128, 128], replicated
- imag_grad: float32 [6, 128, 128], replicated
- gate_grad: float32 [128, 8], replicated
The draws below stay inside these ranges and needn't reach their ends.
Inputs may be any that keep to these rules, and one draw needn't show every extreme that they name: `boundary`: in each round the 16 rows of a partition are distinct. `edge_count`: the live slots are the first ones of a partition's block; some partition has all 192 slots live.
All inputs are finite; a program needn't handle non-finite values.
Results may differ from the reference program's by a relative error of at most 0.0033.
Values may be sent and summed in bfloat16 or wider, within the bound.
A program may use at most 128 MiB of HBM per device.

```python
import jax
import jax.numpy as jnp
import numpy as np
from jax import lax

LMAX = 6
C = 128
H = 8
ROUNDS = 5
NLOC = 32
B = 16
E = 192
COMPS = 49
NODES = 8192
N_DOM = 256


def draw_boundary(key, part):
    key = jax.random.fold_in(key, 11)
    keys = jax.random.split(key, N_DOM * ROUNDS)

    def pick_rows(single):
        return jax.random.permutation(single, NLOC)[:B]
    picks = jax.vmap(pick_rows)(keys)
    return picks.reshape(N_DOM, ROUNDS, B).astype(jnp.int32)


def draw_edge_count(key, part):
    key = jax.random.fold_in(key, 23)
    first, second = jax.random.split(key)
    counts = jax.random.randint(first, (N_DOM,), E // 8, E + 1)
    fullest = jax.random.randint(second, (), 0, N_DOM)
    return counts.at[fullest].set(E).astype(jnp.int32)


def set_ends(values, own_key, smallest, high):
    shape = values.shape
    place = [jax.random.randint(jax.random.fold_in(own_key, axis), (), 0, shape[axis]) for axis in range(len(shape))]
    values = values.at[tuple(place)].set(smallest)
    longest = shape.index(max(shape))
    place[longest] = (place[longest] + 1) % shape[longest]
    return values.at[tuple(place)].set(high)


def shard_levels(stream_key, dims, cuts, least, top_value):
    level, own = 1.0, jax.random.fold_in(stream_key, 6)
    for dim, parts in cuts:
        steps = jnp.exp(jax.random.uniform(jax.random.fold_in(own, dim), (parts,), jnp.float32, least / len(cuts), top_value / len(cuts)))
        level = level * jnp.repeat(steps, dims[dim] // parts).reshape([-1 if axis == dim else 1 for axis in range(len(dims))])
    return level


def scatter_about(key, dims, width, reach, cuts=(), held_as=jnp.bfloat16):
    factor_of = shard_levels(key, dims, cuts, -0.22, 0.18) if cuts else 1.0
    values = jax.random.normal(key, dims, jnp.float32) * width * factor_of
    return jnp.minimum(jnp.maximum(values, -reach), reach).astype(held_as)


def setup_inputs(seed: int = 0) -> dict:
    seeds = jax.random.split(jax.random.key(seed), 11)
    return {
        "node_feats": scatter_about(seeds[0], (NODES, COMPS, C), 1.0, 6.0, ((0, 256),)),
        "cotangent": scatter_about(seeds[1], (NODES, COMPS, C), 1.0, 6.0, ((0, 256),)),
        "boundary": draw_boundary(jax.random.fold_in(seeds[10], 71), 0),
        "edge_src": set_ends(jax.random.randint(seeds[3], (N_DOM, E), 0, NLOC + ROUNDS * B), jax.random.fold_in(seeds[3], 1), 0, (NLOC + ROUNDS * B) - 1).astype(jnp.int32),
        "edge_dst": set_ends(jax.random.randint(seeds[4], (N_DOM, E), 0, NLOC), jax.random.fold_in(seeds[4], 1), 0, NLOC - 1).astype(jnp.int32),
        "edge_dist": jnp.clip(0.5 + 4.0 * jax.random.uniform(seeds[5], (N_DOM, E), jnp.float32) ** shard_levels(seeds[5], (N_DOM, E), ((0, 256),), -0.2, 0.2), 0.5, 4.5),
        "edge_count": draw_edge_count(jax.random.fold_in(seeds[10], 71), 0),
        "w_real": scatter_about(seeds[7], (LMAX + 1, C, C), (2 * C) ** -0.5, 0.375),
        "w_imag": scatter_about(seeds[8], (LMAX, C, C), (2 * C) ** -0.5, 0.375),
        "w_gate": scatter_about(seeds[9], (C, H), C ** -0.5, 0.5),
    }


def component_order(levels):
    listing = []
    for magnitude in range(levels):
        listing += [degree * degree + degree + magnitude for degree in range(magnitude, levels)]
        if magnitude > 0:
            listing += [degree * degree + degree - magnitude for degree in range(magnitude, levels)]
    return np.array(listing, dtype=np.int32)

def apply_weight(feats, weight):
    return jnp.einsum('ekc,cd->ekd', feats.astype(jnp.float32), weight.astype(jnp.float32))

def apply_back(grads, weight):
    return jnp.einsum('ekd,cd->ekc', grads.astype(jnp.float32), weight.astype(jnp.float32))

def outer_sum(feats, grads):
    return jnp.einsum('ekc,ekd->cd', feats.astype(jnp.float32), grads.astype(jnp.float32))

def plane_linear(feats, w_real, w_imag):
    levels = w_real.shape[0]
    pieces = []
    offset = 0
    for magnitude in range(levels):
        count = levels - magnitude
        upper = feats[:, offset:offset + count]
        if magnitude == 0:
            pieces.append(apply_weight(upper, w_real[0]))
            offset += count
        else:
            lower = feats[:, offset + count:offset + 2 * count]
            pieces.append(apply_weight(upper, w_real[magnitude]) - apply_weight(lower, w_imag[magnitude - 1]))
            pieces.append(apply_weight(lower, w_real[magnitude]) + apply_weight(upper, w_imag[magnitude - 1]))
            offset += 2 * count
    return jnp.concatenate(pieces, axis=1)

def plane_linear_grad(feats, grads, w_real, w_imag):
    levels = w_real.shape[0]
    feat_parts = []
    real_parts = []
    imag_parts = []
    offset = 0
    for magnitude in range(levels):
        count = levels - magnitude
        feat_up = feats[:, offset:offset + count]
        grad_up = grads[:, offset:offset + count]
        if magnitude == 0:
            feat_parts.append(apply_back(grad_up, w_real[0]))
            real_parts.append(outer_sum(feat_up, grad_up))
            offset += count
        else:
            feat_low = feats[:, offset + count:offset + 2 * count]
            grad_low = grads[:, offset + count:offset + 2 * count]
            real_w = w_real[magnitude]
            imag_w = w_imag[magnitude - 1]
            feat_parts.append(apply_back(grad_up, real_w) + apply_back(grad_low, imag_w))
            feat_parts.append(apply_back(grad_low, real_w) - apply_back(grad_up, imag_w))
            real_parts.append(outer_sum(feat_up, grad_up) + outer_sum(feat_low, grad_low))
            imag_parts.append(outer_sum(feat_up, grad_low) - outer_sum(feat_low, grad_up))
            offset += 2 * count
    return (jnp.concatenate(feat_parts, axis=1), jnp.stack(real_parts), jnp.stack(imag_parts))

def reference(node_feats, cotangent, boundary, edge_src, edge_dst, edge_dist, edge_count, w_real, w_imag, w_gate):
    levels = LMAX + 1
    order_map = component_order(levels)
    back_map = np.argsort(order_map)
    feats_all = node_feats[:, order_map]
    cot_all = cotangent[:, order_map]
    local_index = jnp.arange(NLOC, dtype=jnp.int32)
    slot_index = jnp.arange(E, dtype=jnp.int32)
    gate_float = w_gate.astype(jnp.float32)

    def device_step(carry, device):
        node_grad, real_acc, imag_acc, gate_acc = carry
        base = device * NLOC
        local_feats = lax.dynamic_slice_in_dim(feats_all, base, NLOC, 0)
        local_cot = lax.dynamic_slice_in_dim(cot_all, base, NLOC, 0)
        pieces = [local_feats]
        ghost_rows = []
        for bit in range(ROUNDS):
            partner = jnp.bitwise_xor(device, jnp.int32(1 << bit))
            rows = (partner * NLOC + boundary[partner, bit]).astype(jnp.int32)
            ghost_rows.append(rows)
            pieces.append(feats_all[rows])
        table = jnp.concatenate(pieces, axis=0)
        sources = edge_src[device]
        targets = edge_dst[device]
        live = (slot_index < edge_count[device]).astype(jnp.float32)
        envelope = (1.0 - edge_dist[device] / 5.0) ** 2
        scale = envelope * live
        edge_feats = table[sources]
        mixed = plane_linear(edge_feats, w_real, w_imag)
        logits = jnp.dot(mixed[:, 0, :], gate_float, precision=lax.Precision.HIGHEST)
        attention = jax.nn.sigmoid(logits)
        spread = jnp.repeat(attention, C // H, axis=1)
        weighting = scale[:, None] * spread
        message = (mixed * weighting[:, None, :]).astype(jnp.bfloat16)
        summed = jnp.zeros((NLOC, COMPS, C), jnp.float32).at[targets].add(message.astype(jnp.float32))
        updated = (local_feats.astype(jnp.float32) + 0.25 * summed).astype(jnp.bfloat16)
        target_cot = local_cot[targets].astype(jnp.float32)
        edge_cot = (target_cot * (0.25 * live)[:, None, None]).astype(jnp.bfloat16)
        cot_float = edge_cot.astype(jnp.float32)
        att_cot = scale[:, None] * lax.optimization_barrier(jnp.sum(cot_float * mixed, axis=1)).reshape(E, H, C // H).sum(axis=2)
        logit_cot = att_cot * attention * (1.0 - attention)
        mixed_cot = cot_float * weighting[:, None, :]
        mixed_cot = mixed_cot.at[:, 0, :].add(jnp.dot(logit_cot, gate_float.T, precision=lax.Precision.HIGHEST))
        mixed_cot = mixed_cot.astype(jnp.bfloat16)
        gate_term = jnp.dot(mixed[:, 0, :].T, logit_cot, precision=lax.Precision.HIGHEST)
        feat_cot, real_term, imag_term = plane_linear_grad(edge_feats, mixed_cot, w_real, w_imag)
        feat_cot = feat_cot.astype(jnp.bfloat16)
        table_cot = jnp.zeros((NLOC + ROUNDS * B, COMPS, C), jnp.float32).at[sources].add(feat_cot.astype(jnp.float32))
        node_grad = node_grad.at[base + local_index].add(table_cot[:NLOC])
        for bit in range(ROUNDS):
            start = NLOC + bit * B
            node_grad = node_grad.at[ghost_rows[bit]].add(table_cot[start:start + B])
        return ((node_grad, real_acc + real_term, imag_acc + imag_term, gate_acc + gate_term), updated)
    init = (cot_all.astype(jnp.float32), jnp.zeros((levels, C, C), jnp.float32), jnp.zeros((LMAX, C, C), jnp.float32), jnp.zeros((C, H), jnp.float32))
    final, updated = lax.scan(device_step, init, jnp.arange(N_DOM, dtype=jnp.int32))
    node_grad, real_grad, imag_grad, gate_grad = final
    updated = updated.reshape(NODES, COMPS, C)[:, back_map]
    return (updated, node_grad[:, back_map], real_grad, imag_grad, gate_grad)
```

```python
import functools

import jax
import jax.numpy as jnp
from jax import lax
from jax.experimental import pallas as pl
from jax.experimental.pallas import tpu as pltpu
from jax.sharding import PartitionSpec as P

MESH = pl.DeviceIdType.MESH
F32 = jnp.float32
BF16 = jnp.bfloat16
HIGHEST = lax.Precision.HIGHEST

LEVELS = 7
SLOT0 = [0, 4, 10, 15, 19, 22, 24, 25]
SLOTS = 25
CHUNKS = [(0, 4), (4, 6), (10, 5), (15, 4), (19, 6)]


def dot(a, b, precision=None):
    return lax.dot_general(
        a, b, (((1,), (0,)), ((), ())), precision=precision, preferred_element_type=F32
    )


def dot_nt(a, b, precision=None):
    return lax.dot_general(
        a, b, (((1,), (1,)), ((), ())), precision=precision, preferred_element_type=F32
    )


def dot_tn(a, b, precision=None):
    return lax.dot_general(
        a, b, (((0,), (0,)), ((), ())), precision=precision, preferred_element_type=F32
    )


def iota(shape, dim):
    return lax.broadcasted_iota(jnp.int32, shape, dim)


def pair_comps(order, i):
    if order == 0:
        la = 2 * i + 1
        lb = 2 * i + 2
        return la * la + la, lb * lb + lb, 1 + i
    deg = i + order
    mid = deg * deg + deg
    return mid + order, mid - order, SLOT0[order] + i


def pair_count(order):
    return 3 if order == 0 else LEVELS - order


def main_kernel(
    nf_hbm, cot_hbm, bnd_ref, src_ref, dst_ref, dist_ref, cnt_ref, wr_ref, wi_ref, wg_ref,
    upd_hbm, ng_hbm, x_hbm,
    nf, cot, upd, ng, table, outgo, back, backin, w256, xbuf, hbuf, ycbuf,
    s_mat, st_mat, d_mat, dt_mat, b_mat, bt_mat, wspread, acc, scale_c,
    in_sem, out_sem, hs_sem, hr_sem, bs_sem, br_sem,
):
    rounds = bnd_ref.shape[1]
    border = bnd_ref.shape[2]
    nloc = nf.shape[1]
    ghosts = rounds * border
    rows = nloc + ghosts
    edges = src_ref.shape[1]
    chans = nf.shape[2]
    heads = wg_ref.shape[0]
    me = lax.axis_index("dom")
    partners = [me + (1 << r) * (1 - 2 * (lax.div(me, 1 << r) % 2)) for r in range(rounds)]

    nf_copy = pltpu.make_async_copy(nf_hbm, nf, in_sem.at[0])
    cot_copy = pltpu.make_async_copy(cot_hbm, cot, in_sem.at[1])
    nf_copy.start()
    cot_copy.start()
    barrier = pltpu.get_barrier_semaphore()
    for p in partners:
        pl.semaphore_signal(barrier, inc=1, device_id=(p,), device_id_type=MESH)

    bnd = bnd_ref[0].astype(F32)
    tiled = dot(bnd, (iota((border, ghosts), 1) % border == iota((border, ghosts), 0)).astype(F32))
    own_round = iota((rounds, ghosts), 1) // border == iota((rounds, ghosts), 0)
    brow = jnp.sum(jnp.where(own_round, tiled, 0.0), axis=0, keepdims=True).astype(jnp.int32)
    bt_mat[...] = (iota((nloc, ghosts), 0) == brow).astype(F32).astype(BF16)
    eye_g = iota((ghosts, ghosts), 0) == iota((ghosts, ghosts), 1)
    bcol = jnp.sum(jnp.where(eye_g, brow, 0).astype(F32), axis=1, keepdims=True).astype(jnp.int32)
    b_mat[...] = (iota((ghosts, nloc), 1) == bcol).astype(F32).astype(BF16)

    nf_copy.wait()
    pl.semaphore_wait(barrier, rounds)

    def lay_out(ca, cb, slot):
        both = jnp.concatenate([nf[ca], nf[cb]], axis=1)
        table[slot, pl.ds(0, nloc), :] = both
        outgo[slot] = dot(b_mat[...], both).astype(BF16)

    def halo(chunk, r):
        first, count = CHUNKS[chunk]
        return pltpu.make_async_remote_copy(
            src_ref=outgo.at[pl.ds(first, count), pl.ds(r * border, border), :],
            dst_ref=table.at[pl.ds(first, count), pl.ds(nloc + r * border, border), :],
            send_sem=hs_sem.at[chunk, r],
            recv_sem=hr_sem.at[chunk, r],
            device_id=(partners[r],),
            device_id_type=MESH,
        )

    def halo_back(chunk, r):
        first, count = CHUNKS[chunk]
        return pltpu.make_async_remote_copy(
            src_ref=back.at[pl.ds(first, count), pl.ds(r * border, border), :],
            dst_ref=backin.at[pl.ds(first, count), pl.ds(r * border, border), :],
            send_sem=bs_sem.at[chunk, r],
            recv_sem=br_sem.at[chunk, r],
            device_id=(partners[r],),
            device_id_type=MESH,
        )

    zero = jnp.zeros((nloc, chans), BF16)
    both = jnp.concatenate([nf[0], zero], axis=1)
    table[0, pl.ds(0, nloc), :] = both
    outgo[0] = dot(b_mat[...], both).astype(BF16)
    chunk_orders = [[0], [1], [2], [3], [4, 5, 6]]
    for chunk, orders in enumerate(chunk_orders):
        for order in orders:

            @pl.loop(0, pair_count(order))
            def _(i, order=order):
                ca, cb, slot = pair_comps(order, i)
                lay_out(ca, cb, slot)

        for r in reversed(range(rounds)):
            halo(chunk, r).start()

    src = src_ref[...]
    dst = dst_ref[...]
    st_mat[...] = (iota((rows, edges), 0) == src).astype(F32).astype(BF16)
    dt_mat[...] = (iota((nloc, edges), 0) == dst).astype(F32).astype(BF16)
    eye = iota((edges, edges), 0) == iota((edges, edges), 1)
    src_col = jnp.sum(jnp.where(eye, src, 0).astype(F32), axis=1, keepdims=True).astype(jnp.int32)
    dst_col = jnp.sum(jnp.where(eye, dst, 0).astype(F32), axis=1, keepdims=True).astype(jnp.int32)
    s_mat[...] = (iota((edges, rows), 1) == src_col).astype(F32).astype(BF16)
    live_col = (iota((edges, 1), 0) < cnt_ref[0]).astype(F32)
    d_mat[...] = jnp.where(iota((edges, nloc), 1) == dst_col, 0.25 * live_col, 0.0).astype(BF16)
    envelope = (1.0 - dist_ref[...] / 5.0) ** 2
    scale_col = jnp.sum(jnp.where(eye, envelope, 0.0), axis=1, keepdims=True) * live_col
    scale_c[...] = jnp.broadcast_to(scale_col, (edges, chans))

    zero_w = jnp.zeros((chans, chans), BF16)
    w256[0] = jnp.concatenate(
        [
            jnp.concatenate([wr_ref[0], zero_w], axis=1),
            jnp.concatenate([zero_w, wr_ref[0]], axis=1),
        ],
        axis=0,
    )
    for m in range(1, LEVELS):
        w256[m] = jnp.concatenate(
            [
                jnp.concatenate([wr_ref[m], wi_ref[m - 1]], axis=1),
                jnp.concatenate([-wi_ref[m - 1], wr_ref[m]], axis=1),
            ],
            axis=0,
        )
    head_of = iota((chans, heads), 0) // (chans // heads) == iota((chans, heads), 1)
    gate_rows = dot(head_of.astype(F32), wg_ref[...].astype(F32))

    cot_copy.wait()
    for r in range(rounds):
        halo(0, r).wait_recv()

    h0 = dot(s_mat[...], table[0, :, pl.ds(0, chans)]).astype(BF16)
    y0 = dot(h0, wr_ref[0])
    att = jax.nn.sigmoid(dot_nt(y0, gate_rows, HIGHEST))
    w_c = scale_c[...] * att
    wspread[:, pl.ds(0, chans)] = w_c
    wspread[:, pl.ds(chans, chans)] = w_c
    u0 = dot(dt_mat[...], (y0 * w_c).astype(BF16))
    upd[0] = (nf[0].astype(F32) + 0.25 * u0).astype(BF16)
    ec0 = dot(d_mat[...], cot[0])
    acc[...] = ec0 * y0

    def pair(order, i):
        ca, cb, slot = pair_comps(order, i)
        h2 = dot(s_mat[...], table[slot]).astype(BF16)
        y2 = dot(h2, w256[order])
        w2 = wspread[...]
        u2 = dot(dt_mat[...], (y2 * w2).astype(BF16))
        upd[ca] = (nf[ca].astype(F32) + 0.25 * u2[:, :chans]).astype(BF16)
        upd[cb] = (nf[cb].astype(F32) + 0.25 * u2[:, chans:]).astype(BF16)
        cot_a = cot[ca]
        cot_b = cot[cb]
        ec2 = dot(d_mat[...], jnp.concatenate([cot_a, cot_b], axis=1))
        prod = ec2 * y2
        acc[...] += prod[:, :chans] + prod[:, chans:]
        yc2 = (ec2 * w2).astype(BF16)
        hc2 = dot_nt(yc2, w256[order]).astype(BF16)
        tc2 = dot(st_mat[...], hc2)
        ng[ca] = cot_a.astype(F32) + tc2[:nloc, :chans]
        ng[cb] = cot_b.astype(F32) + tc2[:nloc, chans:]
        back[slot] = tc2[nloc:].astype(BF16)
        hbuf[pl.ds(i * edges, edges), :] = h2
        ycbuf[pl.ds(i * edges, edges), :] = yc2

    for chunk, orders in enumerate(chunk_orders):
        if chunk > 0:
            for r in range(rounds):
                halo(chunk, r).wait_recv()
        for order in orders:
            n = pair_count(order)

            @pl.loop(0, n)
            def _(i, order=order):
                pair(order, i)

            gw = dot_tn(hbuf[pl.ds(0, n * edges), :], ycbuf[pl.ds(0, n * edges), :])
            xbuf[order, pl.ds(0, chans), :] = gw[:chans, :chans] + gw[chans:, chans:]
            if order > 0:
                xbuf[order, pl.ds(chans, chans), :] = gw[:chans, chans:] - gw[chans:, :chans]
        if chunk > 0:
            for r in reversed(range(rounds)):
                halo_back(chunk, r).start()

    same_head = iota((chans, chans), 0) // (chans // heads) == iota((chans, chans), 1) // (chans // heads)
    att_cot = scale_c[...] * dot(acc[...], same_head.astype(F32), HIGHEST)
    logit_cot = att_cot * att * (1.0 - att)
    head_lead = iota((chans, chans), 0) % (chans // heads) == 0
    yc0 = (ec0 * w_c + dot(logit_cot, jnp.where(head_lead, gate_rows, 0.0), HIGHEST)).astype(BF16)
    hc0 = dot_nt(yc0, wr_ref[0]).astype(BF16)
    tc0 = dot(st_mat[...], hc0)
    ng[0] = cot[0].astype(F32) + tc0[:nloc]
    back[0, :, pl.ds(0, chans)] = tc0[nloc:].astype(BF16)
    back[0, :, pl.ds(chans, chans)] = jnp.zeros((ghosts, chans), BF16)
    for r in reversed(range(rounds)):
        halo_back(0, r).start()
    xbuf[0, pl.ds(0, chans), :] += dot_tn(h0, yc0)
    outer = dot_tn(logit_cot, y0, HIGHEST)
    lead = iota((heads, chans), 1) == iota((heads, chans), 0) * (chans // heads)
    xbuf[0, pl.ds(chans, chans), :] = jnp.zeros((chans, chans), F32)
    xbuf[0, pl.ds(chans, heads), :] = dot(lead.astype(F32), outer, HIGHEST)

    x_copy = pltpu.make_async_copy(xbuf, x_hbm, out_sem.at[0])
    x_copy.start()
    upd_copy = pltpu.make_async_copy(upd, upd_hbm, out_sem.at[1])
    upd_copy.start()

    for chunk in [1, 2, 3, 4, 0]:
        for r in range(rounds):
            halo_back(chunk, r).wait_recv()
        for order in chunk_orders[chunk]:

            @pl.loop(0, pair_count(order))
            def _(i, order=order):
                ca, cb, slot = pair_comps(order, i)
                got = dot(bt_mat[...], backin[slot])
                ng[ca] += got[:, :chans]
                ng[cb] += got[:, chans:]

    ng[0] += dot(bt_mat[...], backin[0, :, pl.ds(0, chans)])
    ng_copy = pltpu.make_async_copy(ng, ng_hbm, out_sem.at[2])
    ng_copy.start()
    for chunk in range(len(CHUNKS)):
        for r in range(rounds):
            halo(chunk, r).wait_send()
            halo_back(chunk, r).wait_send()
    x_copy.wait()
    upd_copy.wait()
    ng_copy.wait()


def reduce_kernel(
    x_ref, real_hbm, imag_hbm, gate_hbm,
    rcore, part, rxy, rz, full, out_sem, cs, xs, xr, zs, zr, gs, gr,
):
    me = lax.axis_index("dom")
    core = me % 2
    xpos = (me // 2) % 4
    zpos = (me // 8) % 8
    ypos = me // 64
    plane = ypos * 4 + xpos
    half = x_ref.shape[1] // 2
    tile = half // 16
    other = me + 1 - 2 * core

    def xy_device(k):
        there = (plane + k) % 16
        return there, (there // 4) * 64 + zpos * 8 + (there % 4) * 2 + core

    def z_device(k):
        return ypos * 64 + ((zpos + k) % 8) * 8 + xpos * 2 + core

    barrier = pltpu.get_barrier_semaphore()
    pl.semaphore_signal(barrier, inc=1, device_id=(other,), device_id_type=MESH)
    for k in range(1, 16):
        pl.semaphore_signal(barrier, inc=1, device_id=(xy_device(k)[1],), device_id_type=MESH)
    for k in range(1, 8):
        pl.semaphore_signal(barrier, inc=1, device_id=(z_device(k),), device_id_type=MESH)
    pl.semaphore_wait(barrier, 1 + 15 + 7)

    mine = pl.ds(pl.multiple_of(core * half, half), half)
    theirs = pl.ds(pl.multiple_of((1 - core) * half, half), half)
    swap = pltpu.make_async_remote_copy(
        src_ref=x_ref.at[:, theirs, :], dst_ref=rcore, send_sem=cs.at[0], recv_sem=cs.at[1],
        device_id=(other,), device_id_type=MESH,
    )
    swap.start()
    swap.wait_recv()
    part[...] = x_ref[:, mine, :] + rcore[...]

    def scatter(k):
        there, device = xy_device(k)
        return pltpu.make_async_remote_copy(
            src_ref=part.at[:, pl.ds(pl.multiple_of(there * tile, tile), tile), :],
            dst_ref=rxy.at[k - 1], send_sem=xs.at[k - 1], recv_sem=xr.at[k - 1],
            device_id=(device,), device_id_type=MESH,
        )

    for k in range(1, 16):
        scatter(k).start()
    own = pl.ds(pl.multiple_of(plane * tile, tile), tile)
    total = part[:, own, :]
    for k in range(1, 16):
        scatter(k).wait_recv()
        total += rxy[k - 1]
    rz[zpos] = total

    def share(k):
        return pltpu.make_async_remote_copy(
            src_ref=rz.at[zpos], dst_ref=rz.at[zpos], send_sem=zs.at[k - 1], recv_sem=zr.at[k - 1],
            device_id=(z_device(k),), device_id_type=MESH,
        )

    def share_in(k):
        slot = (zpos + 8 - k) % 8
        return pltpu.make_async_remote_copy(
            src_ref=rz.at[slot], dst_ref=rz.at[slot], send_sem=zs.at[k - 1], recv_sem=zr.at[k - 1],
            device_id=(z_device(k),), device_id_type=MESH,
        )

    for k in range(1, 8):
        share(k).start()
    for k in range(1, 8):
        share_in(k).wait_recv()
    total = rz[0]
    for k in range(1, 8):
        total += rz[k]
    mine_tile = pl.ds(pl.multiple_of(core * half + plane * tile, tile), tile)
    full[:, mine_tile, :] = total

    def gather(k):
        return pltpu.make_async_remote_copy(
            src_ref=full.at[:, mine_tile, :], dst_ref=full.at[:, mine_tile, :],
            send_sem=gs.at[k - 1], recv_sem=gr.at[k - 1],
            device_id=(xy_device(k)[1],), device_id_type=MESH,
        )

    def gather_in(k):
        source = (plane + 16 - k) % 16
        rows = pl.ds(pl.multiple_of(core * half + source * tile, tile), tile)
        return pltpu.make_async_remote_copy(
            src_ref=full.at[:, rows, :], dst_ref=full.at[:, rows, :],
            send_sem=gs.at[k - 1], recv_sem=gr.at[k - 1],
            device_id=(xy_device(k)[1],), device_id_type=MESH,
        )

    for k in range(1, 16):
        gather(k).start()
    for k in range(1, 16):
        gather_in(k).wait_recv()
    swap_out = pltpu.make_async_remote_copy(
        src_ref=full.at[:, mine, :], dst_ref=full.at[:, mine, :],
        send_sem=cs.at[2], recv_sem=cs.at[3], device_id=(other,), device_id_type=MESH,
    )
    swap_in = pltpu.make_async_remote_copy(
        src_ref=full.at[:, theirs, :], dst_ref=full.at[:, theirs, :],
        send_sem=cs.at[2], recv_sem=cs.at[3], device_id=(other,), device_id_type=MESH,
    )
    swap_out.start()
    swap_in.wait_recv()
    copies = [
        pltpu.make_async_copy(full.at[:, pl.ds(0, half), :], real_hbm, out_sem.at[0]),
        pltpu.make_async_copy(full.at[pl.ds(1, LEVELS - 1), pl.ds(half, half), :], imag_hbm, out_sem.at[1]),
        pltpu.make_async_copy(full.at[0, pl.ds(half, gate_hbm.shape[0]), :], gate_hbm, out_sem.at[2]),
    ]
    for copy in copies:
        copy.start()
    swap.wait_send()
    swap_out.wait_send()
    for k in range(1, 16):
        scatter(k).wait_send()
        gather(k).wait_send()
    for k in range(1, 8):
        share(k).wait_send()
    for copy in copies:
        copy.wait()


def shards(
    node_feats, cotangent, boundary, edge_src, edge_dst, edge_dist, edge_count, w_real, w_imag, w_gate
):
    nloc, comps, chans = node_feats.shape
    rounds, border = boundary.shape[1:]
    edges = edge_src.shape[1]
    heads = w_gate.shape[1]
    ghosts = rounds * border
    rows = nloc + ghosts
    chunks = len(CHUNKS)
    vmem = pl.BlockSpec(memory_space=pltpu.VMEM)
    smem = pl.BlockSpec(memory_space=pltpu.SMEM)
    anywhere = pl.BlockSpec(memory_space=pl.ANY)
    dma = pltpu.SemaphoreType.DMA
    updated, node_grad, x = pl.pallas_call(
        main_kernel,
        out_shape=(
            jax.ShapeDtypeStruct((comps, nloc, chans), BF16),
            jax.ShapeDtypeStruct((comps, nloc, chans), F32),
            jax.ShapeDtypeStruct((LEVELS, 2 * chans, chans), F32),
        ),
        in_specs=[anywhere, anywhere, vmem, vmem, vmem, vmem, smem, vmem, vmem, vmem],
        out_specs=(anywhere, anywhere, anywhere),
        scratch_shapes=[
            pltpu.VMEM((comps, nloc, chans), BF16),
            pltpu.VMEM((comps, nloc, chans), BF16),
            pltpu.VMEM((comps, nloc, chans), BF16),
            pltpu.VMEM((comps, nloc, chans), F32),
            pltpu.VMEM((SLOTS, rows, 2 * chans), BF16),
            pltpu.VMEM((SLOTS, ghosts, 2 * chans), BF16),
            pltpu.VMEM((SLOTS, ghosts, 2 * chans), BF16),
            pltpu.VMEM((SLOTS, ghosts, 2 * chans), BF16),
            pltpu.VMEM((LEVELS, 2 * chans, 2 * chans), BF16),
            pltpu.VMEM((LEVELS, 2 * chans, chans), F32),
            pltpu.VMEM((6 * edges, 2 * chans), BF16),
            pltpu.VMEM((6 * edges, 2 * chans), BF16),
            pltpu.VMEM((edges, rows), BF16),
            pltpu.VMEM((rows, edges), BF16),
            pltpu.VMEM((edges, nloc), BF16),
            pltpu.VMEM((nloc, edges), BF16),
            pltpu.VMEM((ghosts, nloc), BF16),
            pltpu.VMEM((nloc, ghosts), BF16),
            pltpu.VMEM((edges, 2 * chans), F32),
            pltpu.VMEM((edges, chans), F32),
            pltpu.VMEM((edges, chans), F32),
            dma((2,)),
            dma((3,)),
            dma((chunks, rounds)),
            dma((chunks, rounds)),
            dma((chunks, rounds)),
            dma((chunks, rounds)),
        ],
        compiler_params=pltpu.CompilerParams(
            collective_id=0, has_side_effects=True, vmem_limit_bytes=40 * 2**20
        ),
        name="halo_edges",
    )(
        node_feats.transpose(1, 0, 2),
        cotangent.transpose(1, 0, 2),
        boundary,
        edge_src,
        edge_dst,
        edge_dist,
        edge_count,
        w_real,
        w_imag,
        w_gate.T,
    )
    tile = chans // 16
    real, imag, gate = pl.pallas_call(
        reduce_kernel,
        out_shape=(
            jax.ShapeDtypeStruct((LEVELS, chans, chans), F32),
            jax.ShapeDtypeStruct((LEVELS - 1, chans, chans), F32),
            jax.ShapeDtypeStruct((heads, chans), F32),
        ),
        in_specs=[vmem],
        out_specs=(anywhere, anywhere, anywhere),
        scratch_shapes=[
            pltpu.VMEM((LEVELS, chans, chans), F32),
            pltpu.VMEM((LEVELS, chans, chans), F32),
            pltpu.VMEM((15, LEVELS, tile, chans), F32),
            pltpu.VMEM((8, LEVELS, tile, chans), F32),
            pltpu.VMEM((LEVELS, 2 * chans, chans), F32),
            dma((3,)),
            dma((4,)),
            dma((15,)),
            dma((15,)),
            dma((7,)),
            dma((7,)),
            dma((15,)),
            dma((15,)),
        ],
        compiler_params=pltpu.CompilerParams(
            collective_id=1, has_side_effects=True, vmem_limit_bytes=40 * 2**20
        ),
        name="reduce_grads",
    )(x)
    return (updated.transpose(1, 0, 2), node_grad.transpose(1, 0, 2), real, imag, gate.T)


def solution(mesh):
    whole = P("dom", None, None)
    return jax.shard_map(
        shards,
        mesh=mesh,
        in_specs=(
            whole, whole, whole, P("dom", None), P("dom", None), P("dom", None), P("dom"), P(), P(), P(),
        ),
        out_specs=(whole, whole, P(), P(), P()),
        check_vma=False,
    )
```

```python
import functools

import jax
import jax.numpy as jnp
from jax import lax
from jax.experimental import pallas as pl
from jax.experimental.pallas import tpu as pltpu
from jax.sharding import PartitionSpec as P

MESH = pl.DeviceIdType.MESH
F32 = jnp.float32
BF16 = jnp.bfloat16
HIGHEST = lax.Precision.HIGHEST

LEVELS = 7
SLOT0 = [0, 4, 10, 15, 19, 22, 24, 25]
SLOTS = 25
CHUNKS = [(0, 4), (4, 6), (10, 5), (15, 4), (19, 6)]
CHUNK_ORDERS = [[0], [1], [2], [3], [4, 5, 6]]


def dot(a, b, precision=None):
    return lax.dot_general(
        a, b, (((1,), (0,)), ((), ())), precision=precision, preferred_element_type=F32
    )


def dot_nt(a, b, precision=None):
    return lax.dot_general(
        a, b, (((1,), (1,)), ((), ())), precision=precision, preferred_element_type=F32
    )


def dot_tn(a, b, precision=None):
    return lax.dot_general(
        a, b, (((0,), (0,)), ((), ())), precision=precision, preferred_element_type=F32
    )


def iota(shape, dim):
    return lax.broadcasted_iota(jnp.int32, shape, dim)


def pair_comps(order, i):
    if order == 0:
        la = 2 * i + 1
        lb = 2 * i + 2
        return la * la + la, lb * lb + lb, 1 + i
    deg = i + order
    mid = deg * deg + deg
    return mid + order, mid - order, SLOT0[order] + i


def pair_count(order):
    return 3 if order == 0 else LEVELS - order


ALL_PAIRS = [(order, i) for order in range(LEVELS) for i in range(pair_count(order))]


def split(a, axis):
    high = a.astype(BF16)
    low = (a - high.astype(F32)).astype(BF16)
    return jnp.concatenate([high, low], axis=axis)


def main_kernel(
    nf_hbm, cot_hbm, bnd_hbm, src_hbm, dst_hbm, dist_hbm, cnt_hbm, wr_hbm, wi_hbm, wg_hbm,
    upd, ng, xbuf,
    nf, cot, bnd_ref, src_ref, dst_ref, dist_ref, cnt_ref, wr_ref, wi_ref, wg_ref,
    table, outgo, back, backin, w256, vbuf, zbuf, b_mat, bt_mat, kt_mat,
    in_sem, hs_sem, hr_sem, bs_sem, br_sem,
):
    rounds = bnd_ref.shape[0]
    border = bnd_ref.shape[2]
    nloc = nf.shape[1]
    ghosts = rounds * border
    rows = nloc + ghosts
    edges = src_ref.shape[1]
    chans = nf.shape[2]
    heads = wg_ref.shape[0]
    width = chans // heads
    me = lax.axis_index("dom")
    partners = [me + (1 << r) * (1 - 2 * (lax.div(me, 1 << r) % 2)) for r in range(rounds)]

    sources = [bnd_hbm, nf_hbm, src_hbm, dst_hbm, dist_hbm, cnt_hbm, cot_hbm, wr_hbm, wi_hbm, wg_hbm]
    targets = [bnd_ref, nf, src_ref, dst_ref, dist_ref, cnt_ref, cot, wr_ref, wi_ref, wg_ref]
    loads = [
        pltpu.make_async_copy(a, b, in_sem.at[i]) for i, (a, b) in enumerate(zip(sources, targets))
    ]
    for load in loads:
        load.start()
    barrier = pltpu.get_barrier_semaphore()
    for p in partners:
        pl.semaphore_signal(barrier, inc=1, device_id=(p,), device_id_type=MESH)

    loads[0].wait()
    bnd = bnd_ref[:, 0, :].astype(F32)
    tiled = dot(bnd, (iota((border, ghosts), 1) % border == iota((border, ghosts), 0)).astype(F32))
    own_round = iota((rounds, ghosts), 1) // border == iota((rounds, ghosts), 0)
    brow = jnp.sum(jnp.where(own_round, tiled, 0.0), axis=0, keepdims=True).astype(jnp.int32)
    bt = (iota((nloc, ghosts), 0) == brow).astype(F32).astype(BF16)
    bt_mat[...] = bt
    eye = (iota((nloc, nloc), 0) == iota((nloc, nloc), 1)).astype(F32).astype(BF16)
    b_mat[...] = dot_tn(bt, eye).astype(BF16)

    def halo(chunk, r):
        first, count = CHUNKS[chunk]
        return pltpu.make_async_remote_copy(
            src_ref=outgo.at[pl.ds(first, count), pl.ds(r * border, border), :],
            dst_ref=table.at[pl.ds(first, count), pl.ds(nloc + r * border, border), :],
            send_sem=hs_sem.at[chunk, r],
            recv_sem=hr_sem.at[chunk, r],
            device_id=(partners[r],),
            device_id_type=MESH,
        )

    def halo_back(chunk, r):
        first, count = CHUNKS[chunk]
        return pltpu.make_async_remote_copy(
            src_ref=back.at[pl.ds(first, count), pl.ds(r * border, border), :],
            dst_ref=backin.at[pl.ds(first, count), pl.ds(r * border, border), :],
            send_sem=bs_sem.at[chunk, r],
            recv_sem=br_sem.at[chunk, r],
            device_id=(partners[r],),
            device_id_type=MESH,
        )

    loads[1].wait()
    pl.semaphore_wait(barrier, rounds)
    for chunk, orders in enumerate(CHUNK_ORDERS):
        if chunk == 0:
            both = jnp.concatenate([nf[0], jnp.zeros((nloc, chans), BF16)], axis=1)
            table[0, pl.ds(0, nloc), :] = both
            outgo[0] = dot(b_mat[...], both).astype(BF16)
        for order in orders:
            for i in range(pair_count(order)):
                ca, cb, slot = pair_comps(order, i)
                both = jnp.concatenate([nf[ca], nf[cb]], axis=1)
                table[slot, pl.ds(0, nloc), :] = both
                outgo[slot] = dot(b_mat[...], both).astype(BF16)
        for r in reversed(range(rounds)):
            halo(chunk, r).start()

    for load in loads[2:6]:
        load.wait()
    live = (iota((1, edges), 1) < cnt_ref[0]).astype(F32)
    scale = (1.0 - dist_ref[...] / 5.0) ** 2 * live
    scaled = split(jnp.where(iota((rows, edges), 0) == src_ref[...], scale, 0.0), 0)
    into = (iota((nloc, edges), 0) == dst_ref[...]).astype(F32).astype(BF16)
    into2 = jnp.concatenate([into, into], axis=0)
    k2 = dot_nt(scaled, into2)
    k2 = 0.25 * (k2[:rows] + k2[rows:])
    high = k2.astype(BF16).astype(F32)
    k_mat = jnp.where(iota(k2.shape, 1) < nloc, high, k2 - high).astype(BF16)
    kt2 = dot_nt(into2, scaled[:rows]) + dot_nt(into2, scaled[rows:])
    kt2 = 0.25 * kt2
    high = kt2.astype(BF16).astype(F32)
    kt_mat[...] = jnp.where(iota(kt2.shape, 0) < nloc, high, kt2 - high).astype(BF16)

    loads[6].wait()

    def v_of(ca, cb):
        both = jnp.concatenate([cot[ca], cot[cb]], axis=1)
        return dot(k_mat, jnp.concatenate([both, both], axis=0))

    for order, i in ALL_PAIRS:
        ca, cb, slot = pair_comps(order, i)
        vbuf[slot] = v_of(ca, cb)
    v0 = dot(k_mat, jnp.concatenate([cot[0], cot[0]], axis=0))

    for load in loads[7:]:
        load.wait()
    zero_w = jnp.zeros((chans, chans), BF16)
    w256[0] = jnp.concatenate(
        [
            jnp.concatenate([wr_ref[0], zero_w], axis=1),
            jnp.concatenate([zero_w, wr_ref[0]], axis=1),
        ],
        axis=0,
    )
    for m in range(1, LEVELS):
        w256[m] = jnp.concatenate(
            [
                jnp.concatenate([wr_ref[m], wi_ref[m - 1]], axis=1),
                jnp.concatenate([-wi_ref[m - 1], wr_ref[m]], axis=1),
            ],
            axis=0,
        )
    head_of = iota((chans, heads), 0) // width == iota((chans, heads), 1)
    gate_rows = dot(head_of.astype(F32), wg_ref[...].astype(F32)).astype(BF16)

    for r in range(rounds):
        halo(0, r).wait_recv()
    p0 = dot(table[0, :, pl.ds(0, chans)], wr_ref[0])
    att = jax.nn.sigmoid(dot_nt(split(p0, 1), jnp.concatenate([gate_rows, gate_rows], axis=1)))
    att2 = jnp.concatenate([att, att], axis=1)

    def send_back(order):
        n = pair_count(order)
        for i in range(n):
            slot = pair_comps(order, i)[2]
            zbuf[slot] = (att2 * vbuf[slot]).astype(BF16)
        first = pair_comps(order, 0)[2]
        z = zbuf[pl.ds(first, n)].reshape(n * rows, 2 * chans)
        tc = dot_nt(z, w256[order]).reshape(n, rows, 2 * chans)
        for i in range(n):
            ca, cb, slot = pair_comps(order, i)
            ng[ca] = cot[ca].astype(F32) + tc[i, :nloc, :chans]
            ng[cb] = cot[cb].astype(F32) + tc[i, :nloc, chans:]
            back[slot] = tc[i, nloc:].astype(BF16)

    for chunk, orders in enumerate(CHUNK_ORDERS):
        for order in orders:
            send_back(order)
        if chunk > 0:
            for r in reversed(range(rounds)):
                halo_back(chunk, r).start()

    def aggregate(q):
        u = dot(kt_mat[...], q.astype(BF16))
        return u[:nloc] + u[nloc:]

    upd[0] = (nf[0].astype(F32) + aggregate(att * p0)).astype(BF16)
    acc = p0 * v0
    for chunk, orders in enumerate(CHUNK_ORDERS):
        if chunk > 0:
            for r in range(rounds):
                halo(chunk, r).wait_recv()
        for order in orders:
            n = pair_count(order)
            first = pair_comps(order, 0)[2]
            t = table[pl.ds(first, n)].reshape(n * rows, 2 * chans)
            p = dot(t, w256[order]).reshape(n, rows, 2 * chans)
            for i in range(n):
                ca, cb, slot = pair_comps(order, i)
                u = aggregate(att2 * p[i])
                upd[ca] = (nf[ca].astype(F32) + u[:, :chans]).astype(BF16)
                upd[cb] = (nf[cb].astype(F32) + u[:, chans:]).astype(BF16)
                prod = p[i] * vbuf[slot]
                acc += prod[:, :chans] + prod[:, chans:]
            gw = dot_tn(t, zbuf[pl.ds(first, n)].reshape(n * rows, 2 * chans))
            xbuf[order, pl.ds(0, chans), :] = gw[:chans, :chans] + gw[chans:, chans:]
            if order > 0:
                xbuf[order, pl.ds(chans, chans), :] = gw[:chans, chans:] - gw[chans:, :chans]

    same_head = iota((chans, chans), 0) // width == iota((chans, chans), 1) // width
    same_head = same_head.astype(F32).astype(BF16)
    acc = dot(split(acc, 1), jnp.concatenate([same_head, same_head], axis=0))
    logit_cot = acc * att * (1.0 - att)
    lead_rows = jnp.where(iota((chans, chans), 0) % width == 0, gate_rows.astype(F32), 0.0).astype(BF16)
    z0 = att * v0 + dot(split(logit_cot, 1), jnp.concatenate([lead_rows, lead_rows], axis=0))
    z0 = z0.astype(BF16)
    tc0 = dot_nt(z0, wr_ref[0])
    ng[0] = cot[0].astype(F32) + tc0[:nloc]
    back[0] = jnp.concatenate([tc0[nloc:].astype(BF16), jnp.zeros((ghosts, chans), BF16)], axis=1)
    for r in reversed(range(rounds)):
        halo_back(0, r).start()
    xbuf[0, pl.ds(0, chans), :] += dot_tn(table[0, :, pl.ds(0, chans)], z0)
    lead = (iota((heads, chans), 1) == iota((heads, chans), 0) * width).astype(F32)
    xbuf[0, pl.ds(chans, chans), :] = jnp.zeros((chans, chans), F32)
    xbuf[0, pl.ds(chans, heads), :] = dot(lead, dot_tn(logit_cot, p0, HIGHEST), HIGHEST)

    for chunk in [1, 2, 3, 4, 0]:
        for r in range(rounds):
            halo_back(chunk, r).wait_recv()
        for order in CHUNK_ORDERS[chunk]:
            for i in range(pair_count(order)):
                ca, cb, slot = pair_comps(order, i)
                got = dot(bt_mat[...], backin[slot])
                ng[ca] += got[:, :chans]
                ng[cb] += got[:, chans:]
    ng[0] += dot(bt_mat[...], backin[0, :, pl.ds(0, chans)])
    for chunk in range(len(CHUNKS)):
        for r in range(rounds):
            halo(chunk, r).wait_send()
            halo_back(chunk, r).wait_send()


def reduce_kernel(
    x_ref, full,
    rcore, part, rxy, rz, cs, xs, xr, zs, zr, gs, gr,
):
    me = lax.axis_index("dom")
    core = me % 2
    xpos = (me // 2) % 4
    zpos = (me // 8) % 8
    ypos = me // 64
    plane = ypos * 4 + xpos
    half = x_ref.shape[1] // 2
    tile = half // 16
    other = me + 1 - 2 * core

    def xy_device(k):
        there = (plane + k) % 16
        return there, (there // 4) * 64 + zpos * 8 + (there % 4) * 2 + core

    def z_device(k):
        return ypos * 64 + ((zpos + k) % 8) * 8 + xpos * 2 + core

    barrier = pltpu.get_barrier_semaphore()
    pl.semaphore_signal(barrier, inc=1, device_id=(other,), device_id_type=MESH)
    for k in range(1, 16):
        pl.semaphore_signal(barrier, inc=1, device_id=(xy_device(k)[1],), device_id_type=MESH)
    for k in range(1, 8):
        pl.semaphore_signal(barrier, inc=1, device_id=(z_device(k),), device_id_type=MESH)
    pl.semaphore_wait(barrier, 1 + 15 + 7)

    mine = pl.ds(pl.multiple_of(core * half, half), half)
    theirs = pl.ds(pl.multiple_of((1 - core) * half, half), half)
    swap = pltpu.make_async_remote_copy(
        src_ref=x_ref.at[:, theirs, :], dst_ref=rcore, send_sem=cs.at[0], recv_sem=cs.at[1],
        device_id=(other,), device_id_type=MESH,
    )
    swap.start()
    swap.wait_recv()
    part[...] = x_ref[:, mine, :] + rcore[...]

    def scatter(k):
        there, device = xy_device(k)
        return pltpu.make_async_remote_copy(
            src_ref=part.at[:, pl.ds(pl.multiple_of(there * tile, tile), tile), :],
            dst_ref=rxy.at[k - 1], send_sem=xs.at[k - 1], recv_sem=xr.at[k - 1],
            device_id=(device,), device_id_type=MESH,
        )

    for k in range(1, 16):
        scatter(k).start()
    own = pl.ds(pl.multiple_of(plane * tile, tile), tile)
    total = part[:, own, :]
    for k in range(1, 16):
        scatter(k).wait_recv()
        total += rxy[k - 1]
    rz[zpos] = total

    def share(k):
        return pltpu.make_async_remote_copy(
            src_ref=rz.at[zpos], dst_ref=rz.at[zpos], send_sem=zs.at[k - 1], recv_sem=zr.at[k - 1],
            device_id=(z_device(k),), device_id_type=MESH,
        )

    def share_in(k):
        slot = (zpos + 8 - k) % 8
        return pltpu.make_async_remote_copy(
            src_ref=rz.at[slot], dst_ref=rz.at[slot], send_sem=zs.at[k - 1], recv_sem=zr.at[k - 1],
            device_id=(z_device(k),), device_id_type=MESH,
        )

    for k in range(1, 8):
        share(k).start()
    for k in range(1, 8):
        share_in(k).wait_recv()
    total = rz[0]
    for k in range(1, 8):
        total += rz[k]
    mine_tile = pl.ds(pl.multiple_of(core * half + plane * tile, tile), tile)
    full[:, mine_tile, :] = total

    def gather(k):
        return pltpu.make_async_remote_copy(
            src_ref=full.at[:, mine_tile, :], dst_ref=full.at[:, mine_tile, :],
            send_sem=gs.at[k - 1], recv_sem=gr.at[k - 1],
            device_id=(xy_device(k)[1],), device_id_type=MESH,
        )

    def gather_in(k):
        source = (plane + 16 - k) % 16
        rows = pl.ds(pl.multiple_of(core * half + source * tile, tile), tile)
        return pltpu.make_async_remote_copy(
            src_ref=full.at[:, rows, :], dst_ref=full.at[:, rows, :],
            send_sem=gs.at[k - 1], recv_sem=gr.at[k - 1],
            device_id=(xy_device(k)[1],), device_id_type=MESH,
        )

    for k in range(1, 16):
        gather(k).start()
    for k in range(1, 16):
        gather_in(k).wait_recv()
    swap_out = pltpu.make_async_remote_copy(
        src_ref=full.at[:, mine, :], dst_ref=full.at[:, mine, :],
        send_sem=cs.at[2], recv_sem=cs.at[3], device_id=(other,), device_id_type=MESH,
    )
    swap_in = pltpu.make_async_remote_copy(
        src_ref=full.at[:, theirs, :], dst_ref=full.at[:, theirs, :],
        send_sem=cs.at[2], recv_sem=cs.at[3], device_id=(other,), device_id_type=MESH,
    )
    swap_out.start()
    swap_in.wait_recv()
    swap.wait_send()
    swap_out.wait_send()
    for k in range(1, 16):
        scatter(k).wait_send()
        gather(k).wait_send()
    for k in range(1, 8):
        share(k).wait_send()


def store_kernel(upd, ng, full, upd_hbm, ng_hbm, real_hbm, imag_hbm, gate_hbm, sem):
    chans = real_hbm.shape[1]
    copies = [
        pltpu.make_async_copy(ng, ng_hbm, sem.at[0]),
        pltpu.make_async_copy(upd, upd_hbm, sem.at[1]),
        pltpu.make_async_copy(full.at[:, pl.ds(0, chans), :], real_hbm, sem.at[2]),
        pltpu.make_async_copy(full.at[pl.ds(1, LEVELS - 1), pl.ds(chans, chans), :], imag_hbm, sem.at[3]),
        pltpu.make_async_copy(full.at[0, pl.ds(chans, gate_hbm.shape[0]), :], gate_hbm, sem.at[4]),
    ]
    for copy in copies:
        copy.start()
    for copy in copies:
        copy.wait()


def shards(
    node_feats, cotangent, boundary, edge_src, edge_dst, edge_dist, edge_count, w_real, w_imag, w_gate
):
    nloc, comps, chans = node_feats.shape
    rounds, border = boundary.shape[1:]
    edges = edge_src.shape[1]
    heads = w_gate.shape[1]
    ghosts = rounds * border
    rows = nloc + ghosts
    chunks = len(CHUNKS)
    vmem = pl.BlockSpec(memory_space=pltpu.VMEM)
    hbm = pl.BlockSpec(memory_space=pltpu.HBM)
    dma = pltpu.SemaphoreType.DMA
    inputs = (
        node_feats.transpose(1, 0, 2),
        cotangent.transpose(1, 0, 2),
        boundary.transpose(1, 0, 2),
        edge_src,
        edge_dst,
        edge_dist,
        edge_count,
        w_real,
        w_imag,
        w_gate.T,
    )
    order = [0, 1, 2, 3, 4, 5, 6, 7, 8, 9]
    held = [
        (pltpu.SMEM if i == 6 else pltpu.VMEM)(inputs[i].shape, inputs[i].dtype) for i in order
    ]
    updated, node_grad, x = pl.pallas_call(
        main_kernel,
        out_shape=(
            jax.ShapeDtypeStruct((comps, nloc, chans), BF16),
            jax.ShapeDtypeStruct((comps, nloc, chans), F32),
            jax.ShapeDtypeStruct((LEVELS, 2 * chans, chans), F32),
        ),
        in_specs=[hbm] * len(inputs),
        out_specs=(vmem, vmem, vmem),
        scratch_shapes=held + [
            pltpu.VMEM((SLOTS, rows, 2 * chans), BF16),
            pltpu.VMEM((SLOTS, ghosts, 2 * chans), BF16),
            pltpu.VMEM((SLOTS, ghosts, 2 * chans), BF16),
            pltpu.VMEM((SLOTS, ghosts, 2 * chans), BF16),
            pltpu.VMEM((LEVELS, 2 * chans, 2 * chans), BF16),
            pltpu.VMEM((SLOTS, rows, 2 * chans), F32),
            pltpu.VMEM((SLOTS, rows, 2 * chans), BF16),
            pltpu.VMEM((ghosts, nloc), BF16),
            pltpu.VMEM((nloc, ghosts), BF16),
            pltpu.VMEM((2 * nloc, rows), BF16),
            dma((len(inputs),)),
            dma((chunks, rounds)),
            dma((chunks, rounds)),
            dma((chunks, rounds)),
            dma((chunks, rounds)),
        ],
        compiler_params=pltpu.CompilerParams(
            collective_id=0, has_side_effects=True, vmem_limit_bytes=40 * 2**20
        ),
        name="halo_edges",
    )(*inputs)
    tile = chans // 16
    full = pl.pallas_call(
        reduce_kernel,
        out_shape=jax.ShapeDtypeStruct((LEVELS, 2 * chans, chans), F32),
        in_specs=[vmem],
        out_specs=vmem,
        scratch_shapes=[
            pltpu.VMEM((LEVELS, chans, chans), F32),
            pltpu.VMEM((LEVELS, chans, chans), F32),
            pltpu.VMEM((15, LEVELS, tile, chans), F32),
            pltpu.VMEM((8, LEVELS, tile, chans), F32),
            dma((4,)),
            dma((15,)),
            dma((15,)),
            dma((7,)),
            dma((7,)),
            dma((15,)),
            dma((15,)),
        ],
        compiler_params=pltpu.CompilerParams(
            collective_id=1, has_side_effects=True, vmem_limit_bytes=40 * 2**20
        ),
        name="reduce_grads",
    )(x)
    updated, node_grad, real, imag, gate = pl.pallas_call(
        store_kernel,
        out_shape=(
            jax.ShapeDtypeStruct((comps, nloc, chans), BF16),
            jax.ShapeDtypeStruct((comps, nloc, chans), F32),
            jax.ShapeDtypeStruct((LEVELS, chans, chans), F32),
            jax.ShapeDtypeStruct((LEVELS - 1, chans, chans), F32),
            jax.ShapeDtypeStruct((heads, chans), F32),
        ),
        in_specs=[vmem] * 3,
        out_specs=(hbm,) * 5,
        scratch_shapes=[dma((5,))],
        name="store",
    )(updated, node_grad, full)
    return (updated.transpose(1, 0, 2), node_grad.transpose(1, 0, 2), real, imag, gate.T)


def solution(mesh):
    whole = P("dom", None, None)
    return jax.shard_map(
        shards,
        mesh=mesh,
        in_specs=(
            whole, whole, whole, P("dom", None), P("dom", None), P("dom", None), P("dom"), P(), P(), P(),
        ),
        out_specs=(whole, whole, P(), P(), P()),
        check_vma=False,
    )
```

```python
import functools

import jax
import jax.numpy as jnp
from jax import lax
from jax.experimental import pallas as pl
from jax.experimental.pallas import tpu as pltpu
from jax.sharding import PartitionSpec as P

MESH = pl.DeviceIdType.MESH
F32 = jnp.float32
BF16 = jnp.bfloat16
HIGHEST = lax.Precision.HIGHEST

LEVELS = 7
SLOT0 = [0, 4, 10, 15, 19, 22, 24, 25]
SLOTS = 25
CHUNKS = [(0, 4), (19, 6), (15, 4), (10, 5), (4, 6)]
CHUNK_ORDERS = [[0], [4, 5, 6], [3], [2], [1]]
EARLY = (2, 5)
LATE = (0, 2)


def dot(a, b, precision=None):
    return lax.dot_general(
        a, b, (((1,), (0,)), ((), ())), precision=precision, preferred_element_type=F32
    )


def dot_nt(a, b, precision=None):
    return lax.dot_general(
        a, b, (((1,), (1,)), ((), ())), precision=precision, preferred_element_type=F32
    )


def dot_tn(a, b, precision=None):
    return lax.dot_general(
        a, b, (((0,), (0,)), ((), ())), precision=precision, preferred_element_type=F32
    )


def iota(shape, dim):
    return lax.broadcasted_iota(jnp.int32, shape, dim)


def pair_comps(order, i):
    if order == 0:
        la = 2 * i + 1
        lb = 2 * i + 2
        return la * la + la, lb * lb + lb, 1 + i
    deg = i + order
    mid = deg * deg + deg
    return mid + order, mid - order, SLOT0[order] + i


def pair_count(order):
    return 3 if order == 0 else LEVELS - order


ALL_PAIRS = [(order, i) for order in range(LEVELS) for i in range(pair_count(order))]


def split(a, axis):
    high = a.astype(BF16)
    low = (a - high.astype(F32)).astype(BF16)
    return jnp.concatenate([high, low], axis=axis)


def place(order):
    return (order + LEVELS - 1) % LEVELS


def remote(src, dst, send_sem, recv_sem, device):
    return pltpu.make_async_remote_copy(
        src_ref=src, dst_ref=dst, send_sem=send_sem, recv_sem=recv_sem,
        device_id=(device,), device_id_type=MESH,
    )


def main_kernel(
    nf_hbm, cot_hbm, bnd_hbm, src_hbm, dst_hbm, dist_hbm, cnt_hbm, wr_hbm, wi_hbm, wg_hbm,
    upd, ng, full, gate,
    nf, cot, bnd_ref, src_ref, dst_ref, dist_ref, cnt_ref, wr_ref, wi_ref, wg_ref,
    pairs, vout, vin, vown, qout, table, pbuf, w256, xbuf, rcore, part, rxy, rz, mine_m, m_xy, m_z, m_core,
    in_sem, vs_sem, vr_sem, qs_sem, qr_sem, core_sem, xs_sem, xr_sem, zs_sem, zr_sem, gs_sem, gr_sem,
    bs_sem, br_sem, cs_sem, cr_sem,
):
    rounds = bnd_ref.shape[0]
    border = bnd_ref.shape[2]
    nloc = nf.shape[1]
    ghosts = rounds * border
    rows = nloc + ghosts
    edges = src_ref.shape[1]
    chans = nf.shape[2]
    heads = wg_ref.shape[0]
    width = chans // heads
    me = lax.axis_index("dom")
    core = me % 2
    xpos = (me // 2) % 4
    zpos = (me // 8) % 8
    ypos = me // 64
    plane = ypos * 4 + xpos
    half = chans
    tile = half // 16
    partners = [me + (1 << r) * (1 - 2 * ((me // (1 << r)) % 2)) for r in range(rounds)]
    other = partners[0]
    xy = [(plane + k) % 16 for k in range(16)]
    xy_from = [(plane + 16 - k) % 16 for k in range(16)]
    xy_device = [(j // 4) * 64 + zpos * 8 + (j % 4) * 2 + core for j in xy]
    z_from = [(zpos + 8 - k) % 8 for k in range(8)]
    z_device = [ypos * 64 + ((zpos + k) % 8) * 8 + xpos * 2 + core for k in range(8)]

    sources = [bnd_hbm, cot_hbm, src_hbm, dst_hbm, dist_hbm, cnt_hbm, nf_hbm, wr_hbm, wi_hbm, wg_hbm]
    targets = [bnd_ref, cot, src_ref, dst_ref, dist_ref, cnt_ref, nf, wr_ref, wi_ref, wg_ref]
    loads = [
        pltpu.make_async_copy(a, b, in_sem.at[i]) for i, (a, b) in enumerate(zip(sources, targets))
    ]
    for load in loads:
        load.start()
    barrier = pltpu.get_barrier_semaphore()
    peers = [other] + xy_device[1:] + z_device[1:]
    for device in peers:
        pl.semaphore_signal(barrier, inc=1, device_id=(device,), device_id_type=MESH)

    loads[0].wait()
    bnd = bnd_ref[:, 0, :].astype(F32)
    tiled = dot(bnd, (iota((border, ghosts), 1) % border == iota((border, ghosts), 0)).astype(F32))
    own_round = iota((rounds, ghosts), 1) // border == iota((rounds, ghosts), 0)
    brow = jnp.sum(jnp.where(own_round, tiled, 0.0), axis=0, keepdims=True).astype(jnp.int32)
    bt = (iota((nloc, ghosts), 0) == brow).astype(F32).astype(BF16)
    eye = (iota((nloc, nloc), 0) == iota((nloc, nloc), 1)).astype(F32).astype(BF16)
    b = dot_tn(bt, eye).astype(BF16)

    for load in loads[1:6]:
        load.wait()
    live = (iota((1, edges), 1) < cnt_ref[0]).astype(F32)
    scale = (1.0 - dist_ref[...] / 5.0) ** 2 * live
    scaled = split(jnp.where(iota((rows, edges), 0) == src_ref[...], scale, 0.0), 0)
    into = (iota((nloc, edges), 0) == dst_ref[...]).astype(F32).astype(BF16)
    into2 = jnp.concatenate([into, into], axis=0)
    k2 = dot_nt(scaled, into2)
    k2 = 0.25 * (k2[:rows] + k2[rows:])
    high = k2.astype(BF16).astype(F32)
    k_mat = jnp.where(iota(k2.shape, 1) < nloc, high, k2 - high).astype(BF16)
    kt2 = dot_nt(into2, scaled[:rows]) + dot_nt(into2, scaled[rows:])
    kt2 = 0.25 * kt2
    high = kt2.astype(BF16).astype(F32)
    kt_mat = jnp.where(iota(kt2.shape, 0) < nloc, high, kt2 - high).astype(BF16)

    def v_halo(chunk, r):
        first, count = CHUNKS[chunk]
        at = (pl.ds(first, count), pl.ds(r * border, border), slice(None))
        return remote(vout.at[at], vin.at[at], vs_sem.at[chunk, r], vr_sem.at[chunk, r], partners[r])

    def q_halo(chunk, r):
        first, count = CHUNKS[chunk]
        return remote(
            qout.at[pl.ds(first, count), pl.ds(r * border, border), :],
            table.at[pl.ds(first, count), pl.ds(nloc + r * border, border), :],
            qs_sem.at[chunk, r], qr_sem.at[chunk, r], partners[r],
        )

    for chunk, orders in enumerate(CHUNK_ORDERS):
        if chunk == 0:
            v = dot(k_mat, jnp.concatenate([cot[0], cot[0]], axis=0))
            v = jnp.concatenate([v, jnp.zeros((rows, chans), F32)], axis=1)
            vown[0] = v[:nloc]
            vout[0] = v[nloc:].astype(BF16)
        for order in orders:
            for i in range(pair_count(order)):
                ca, cb, slot = pair_comps(order, i)
                both = jnp.concatenate([cot[ca], cot[cb]], axis=1)
                v = dot(k_mat, jnp.concatenate([both, both], axis=0))
                vown[slot] = v[:nloc]
                vout[slot] = v[nloc:].astype(BF16)
        if chunk == 0:
            pl.semaphore_wait(barrier, len(peers))
        for r in reversed(range(rounds)):
            v_halo(chunk, r).start()

    for load in loads[6:]:
        load.wait()
    zero_w = jnp.zeros((chans, chans), BF16)
    w256[0] = jnp.concatenate(
        [
            jnp.concatenate([wr_ref[0], zero_w], axis=1),
            jnp.concatenate([zero_w, wr_ref[0]], axis=1),
        ],
        axis=0,
    )
    for m in range(1, LEVELS):
        w256[m] = jnp.concatenate(
            [
                jnp.concatenate([wr_ref[m], wi_ref[m - 1]], axis=1),
                jnp.concatenate([-wi_ref[m - 1], wr_ref[m]], axis=1),
            ],
            axis=0,
        )
    head_of = iota((chans, heads), 0) // width == iota((chans, heads), 1)
    gate_rows = dot(head_of.astype(F32), wg_ref[...].astype(F32)).astype(BF16)

    p0 = dot(nf[0], wr_ref[0])
    att = jax.nn.sigmoid(dot_nt(split(p0, 1), jnp.concatenate([gate_rows, gate_rows], axis=1)))
    att2 = jnp.concatenate([att, att], axis=1)
    q = jnp.concatenate([att * p0, jnp.zeros((nloc, chans), F32)], axis=1).astype(BF16)
    table[0, pl.ds(0, nloc), :] = q
    qout[0] = dot(b, q).astype(BF16)
    for chunk, orders in enumerate(CHUNK_ORDERS):
        for order in orders:
            n = pair_count(order)
            first = pair_comps(order, 0)[2]
            for i in range(n):
                ca, cb, slot = pair_comps(order, i)
                pairs[slot] = jnp.concatenate([nf[ca], nf[cb]], axis=1)
            p = dot(pairs[pl.ds(first, n)].reshape(n * nloc, 2 * chans), w256[order])
            p = p.reshape(n, nloc, 2 * chans)
            pbuf[pl.ds(first, n)] = p
            for i in range(n):
                q = (att2 * p[i]).astype(BF16)
                table[first + i, pl.ds(0, nloc), :] = q
                qout[first + i] = dot(b, q).astype(BF16)
        for r in reversed(range(rounds)):
            q_halo(chunk, r).start()

    def rows_of(core_half, j):
        return pl.ds(pl.multiple_of(core_half * half + j * tile, tile), tile)

    mine = pl.ds(pl.multiple_of(core * half, half), half)
    theirs = pl.ds(pl.multiple_of((1 - core) * half, half), half)

    def swap(batch):
        first, n = batch
        s = 0 if batch is EARLY else 2
        at = pl.ds(first, n)
        return remote(xbuf.at[at, theirs, :], rcore.at[at], core_sem.at[s], core_sem.at[s + 1], other)

    def scatter(batch, k):
        first, n = batch
        s = 0 if batch is EARLY else 1
        at = pl.ds(first, n)
        own = pl.ds(pl.multiple_of(xy[k] * tile, tile), tile)
        return remote(
            part.at[at, own, :], rxy.at[k - 1, at], xs_sem.at[s, k - 1], xr_sem.at[s, k - 1], xy_device[k]
        )

    def share(batch, k, slot):
        first, n = batch
        s = 0 if batch is EARLY else 1
        ref = rz.at[slot, pl.ds(first, n)]
        return remote(ref, ref, zs_sem.at[s, k - 1], zr_sem.at[s, k - 1], z_device[k])

    def gather(batch, k, j):
        first, n = batch
        s = 0 if batch is EARLY else 1
        ref = full.at[pl.ds(first, n), rows_of(core, j), :]
        return remote(ref, ref, gs_sem.at[s, k - 1], gr_sem.at[s, k - 1], xy_device[k])

    def swap_back(batch, rows_half):
        first, n = batch
        s = 4 if batch is EARLY else 6
        ref = full.at[pl.ds(first, n), rows_half, :]
        return remote(ref, ref, core_sem.at[s], core_sem.at[s + 1], other)

    def after_swap(batch):
        swap(batch).wait_recv()
        at = pl.ds(batch[0], batch[1])
        part[at] = xbuf[at, mine, :] + rcore[at]
        for k in range(1, 16):
            scatter(batch, k).start()

    def after_scatter(batch):
        at = pl.ds(batch[0], batch[1])
        total = part[at, pl.ds(pl.multiple_of(plane * tile, tile), tile), :]
        for k in range(1, 16):
            scatter(batch, k).wait_recv()
            total += rxy[k - 1, at]
        rz[zpos, at] = total
        for k in range(1, 8):
            share(batch, k, zpos).start()

    def after_share(batch):
        at = pl.ds(batch[0], batch[1])
        for k in range(1, 8):
            share(batch, k, z_from[k]).wait_recv()
        total = rz[0, at]
        for k in range(1, 8):
            total += rz[k, at]
        full[at, rows_of(core, plane), :] = total
        for k in range(1, 16):
            gather(batch, k, plane).start()

    def after_gather(batch):
        for k in range(1, 16):
            gather(batch, k, xy_from[k]).wait_recv()
        swap_back(batch, mine).start()

    v0 = None
    acc = None
    xbuf[place(0), pl.ds(chans, chans), :] = jnp.zeros((chans, chans), F32)
    for chunk, orders in enumerate(CHUNK_ORDERS):
        for r in range(rounds):
            v_halo(chunk, r).wait_recv()
        if chunk == 0:
            v0 = vown[0, :, pl.ds(0, chans)] + dot(bt, vin[0, :, pl.ds(0, chans)])
            acc = p0 * v0
        for order in orders:
            n = pair_count(order)
            first = pair_comps(order, 0)[2]
            z = []
            for i in range(n):
                v = vown[first + i] + dot(bt, vin[first + i])
                prod = pbuf[first + i] * v
                acc += prod[:, :chans] + prod[:, chans:]
                z.append(att2 * v)
            z = jnp.concatenate(z, axis=0)
            high = z.astype(BF16)
            low = (z - high.astype(F32)).astype(BF16)
            tc = dot_nt(high, w256[order]).reshape(n, nloc, 2 * chans)
            for i in range(n):
                ca, cb, slot = pair_comps(order, i)
                ng[ca] = cot[ca].astype(F32) + tc[i, :, :chans]
                ng[cb] = cot[cb].astype(F32) + tc[i, :, chans:]
            t = pairs[pl.ds(first, n)].reshape(n * nloc, 2 * chans)
            gw = dot_tn(jnp.concatenate([t, t], axis=0), jnp.concatenate([high, low], axis=0))
            real = gw[:chans, :chans] + gw[chans:, chans:]
            if order == 0:
                real += dot_tn(jnp.concatenate([nf[0], nf[0]], axis=0), split(att * v0, 0))
            else:
                xbuf[place(order), pl.ds(chans, chans), :] = gw[:chans, chans:] - gw[chans:, :chans]
            xbuf[place(order), pl.ds(0, chans), :] = real
        if chunk == 2:
            swap(EARLY).start()
        if chunk == 3:
            after_swap(EARLY)
    swap(LATE).start()

    same_head = iota((chans, chans), 0) // width == iota((chans, chans), 1) // width
    same_head = same_head.astype(F32).astype(BF16)
    acc = dot(split(acc, 1), jnp.concatenate([same_head, same_head], axis=0))
    logit_cot = acc * att * (1.0 - att)
    lead = (iota((heads, chans), 1) == iota((heads, chans), 0) * width).astype(F32)
    outer = dot_tn(split(logit_cot, 0), jnp.concatenate([nf[0], nf[0]], axis=0))
    m_xy[plane] = dot(lead, outer, HIGHEST)

    def m_share(k, j):
        return remote(m_xy.at[j], m_xy.at[j], bs_sem.at[k - 1], br_sem.at[k - 1], xy_device[k])

    def m_share_z(k, slot):
        return remote(m_z.at[slot], m_z.at[slot], cs_sem.at[k - 1], cr_sem.at[k - 1], z_device[k])

    for k in range(1, 16):
        m_share(k, plane).start()
    after_swap(LATE)
    lead_rows = jnp.where(iota((chans, chans), 0) % width == 0, gate_rows.astype(F32), 0.0).astype(BF16)
    z0 = att * v0 + dot(split(logit_cot, 1), jnp.concatenate([lead_rows, lead_rows], axis=0))
    ng[0] = cot[0].astype(F32) + dot_nt(z0.astype(BF16), wr_ref[0])

    after_scatter(EARLY)
    for k in range(1, 16):
        m_share(k, xy_from[k]).wait_recv()
    total = m_xy[0]
    for j in range(1, 16):
        total += m_xy[j]
    m_z[zpos] = total
    for k in range(1, 8):
        m_share_z(k, zpos).start()
    after_scatter(LATE)
    after_share(EARLY)

    def aggregate(q):
        u = dot(kt_mat, q)
        return u[:nloc] + u[nloc:]

    def forward(chunk):
        for r in range(rounds):
            q_halo(chunk, r).wait_recv()
        if chunk == 0:
            upd[0] = (nf[0].astype(F32) + aggregate(table[0, :, pl.ds(0, chans)])).astype(BF16)
        for order in CHUNK_ORDERS[chunk]:
            for i in range(pair_count(order)):
                ca, cb, slot = pair_comps(order, i)
                u = aggregate(table[slot])
                upd[ca] = (nf[ca].astype(F32) + u[:, :chans]).astype(BF16)
                upd[cb] = (nf[cb].astype(F32) + u[:, chans:]).astype(BF16)

    forward(0)
    forward(1)
    for k in range(1, 8):
        m_share_z(k, z_from[k]).wait_recv()
    total = m_z[0]
    for j in range(1, 8):
        total += m_z[j]
    mine_m[...] = total
    m_swap = remote(mine_m, m_core, core_sem.at[8], core_sem.at[9], other)
    m_swap.start()
    after_share(LATE)
    forward(2)
    after_gather(EARLY)
    forward(3)
    forward(4)
    m_swap.wait_recv()
    m_total = mine_m[...] + m_core[...]
    w0 = wr_ref[0]
    gate[...] = dot(split(m_total, 1), jnp.concatenate([w0, w0], axis=0))
    wg = wg_ref[...].astype(F32)
    late_real = dot_tn(split(m_total, 0), jnp.concatenate([wg, wg], axis=0).astype(BF16))
    swap_back(EARLY, theirs).wait_recv()
    swap_back(EARLY, mine).wait_send()
    for k in range(1, 16):
        gather(EARLY, k, plane).wait_send()
    full[place(0), pl.ds(0, chans), :] += late_real
    after_gather(LATE)
    swap_back(LATE, theirs).wait_recv()

    swap_back(LATE, mine).wait_send()
    m_swap.wait_send()
    for chunk in range(len(CHUNKS)):
        for r in range(rounds):
            v_halo(chunk, r).wait_send()
            q_halo(chunk, r).wait_send()
    for batch in (EARLY, LATE):
        swap(batch).wait_send()
        for k in range(1, 16):
            scatter(batch, k).wait_send()
            if batch is LATE:
                gather(batch, k, plane).wait_send()
        for k in range(1, 8):
            share(batch, k, zpos).wait_send()
    for k in range(1, 16):
        m_share(k, plane).wait_send()
    for k in range(1, 8):
        m_share_z(k, zpos).wait_send()


def store_kernel(upd, ng, full, gate, upd_hbm, ng_hbm, real_hbm, imag_hbm, gate_hbm, sem):
    chans = real_hbm.shape[1]
    above = LEVELS - 1
    copies = [
        (ng, ng_hbm),
        (upd, upd_hbm),
        (full.at[pl.ds(0, above), pl.ds(0, chans), :], real_hbm.at[pl.ds(1, above)]),
        (full.at[pl.ds(0, above), pl.ds(chans, chans), :], imag_hbm),
        (full.at[above, pl.ds(0, chans), :], real_hbm.at[0]),
        (gate, gate_hbm),
    ]
    copies = [pltpu.make_async_copy(a, b, sem.at[i]) for i, (a, b) in enumerate(copies)]
    for copy in copies:
        copy.start()
    for copy in copies:
        copy.wait()


def shards(
    node_feats, cotangent, boundary, edge_src, edge_dst, edge_dist, edge_count, w_real, w_imag, w_gate
):
    nloc, comps, chans = node_feats.shape
    rounds, border = boundary.shape[1:]
    heads = w_gate.shape[1]
    ghosts = rounds * border
    rows = nloc + ghosts
    chunks = len(CHUNKS)
    pair = 2 * chans
    tile = chans // 16
    vmem = pl.BlockSpec(memory_space=pltpu.VMEM)
    hbm = pl.BlockSpec(memory_space=pltpu.HBM)
    dma = pltpu.SemaphoreType.DMA
    inputs = (
        node_feats.transpose(1, 0, 2),
        cotangent.transpose(1, 0, 2),
        boundary.transpose(1, 0, 2),
        edge_src,
        edge_dst,
        edge_dist,
        edge_count,
        w_real,
        w_imag,
        w_gate.T,
    )
    inputs = [
        a if a.ndim == 1 else pltpu.with_memory_space_constraint(a, pltpu.HBM) for a in inputs
    ]
    held = [
        (pltpu.SMEM if i == 6 else pltpu.VMEM)(a.shape, a.dtype) for i, a in enumerate(inputs)
    ]
    updated, node_grad, full, gate = pl.pallas_call(
        main_kernel,
        out_shape=(
            jax.ShapeDtypeStruct((comps, nloc, chans), BF16),
            jax.ShapeDtypeStruct((comps, nloc, chans), F32),
            jax.ShapeDtypeStruct((LEVELS, pair, chans), F32),
            jax.ShapeDtypeStruct((heads, chans), F32),
        ),
        in_specs=[hbm] * len(inputs),
        out_specs=(vmem,) * 4,
        scratch_shapes=held + [
            pltpu.VMEM((SLOTS, nloc, pair), BF16),
            pltpu.VMEM((SLOTS, ghosts, pair), BF16),
            pltpu.VMEM((SLOTS, ghosts, pair), BF16),
            pltpu.VMEM((SLOTS, nloc, pair), F32),
            pltpu.VMEM((SLOTS, ghosts, pair), BF16),
            pltpu.VMEM((SLOTS, rows, pair), BF16),
            pltpu.VMEM((SLOTS, nloc, pair), F32),
            pltpu.VMEM((LEVELS, pair, pair), BF16),
            pltpu.VMEM((LEVELS, pair, chans), F32),
            pltpu.VMEM((LEVELS, chans, chans), F32),
            pltpu.VMEM((LEVELS, chans, chans), F32),
            pltpu.VMEM((15, LEVELS, tile, chans), F32),
            pltpu.VMEM((8, LEVELS, tile, chans), F32),
            pltpu.VMEM((heads, chans), F32),
            pltpu.VMEM((16, heads, chans), F32),
            pltpu.VMEM((8, heads, chans), F32),
            pltpu.VMEM((heads, chans), F32),
            dma((len(inputs),)),
            dma((chunks, rounds)),
            dma((chunks, rounds)),
            dma((chunks, rounds)),
            dma((chunks, rounds)),
            dma((10,)),
            dma((2, 15)),
            dma((2, 15)),
            dma((2, 7)),
            dma((2, 7)),
            dma((2, 15)),
            dma((2, 15)),
            dma((15,)),
            dma((15,)),
            dma((7,)),
            dma((7,)),
        ],
        compiler_params=pltpu.CompilerParams(
            collective_id=0, has_side_effects=True, vmem_limit_bytes=40 * 2**20
        ),
        name="halo_edges",
    )(*inputs)
    updated, node_grad, real, imag, gate = pl.pallas_call(
        store_kernel,
        out_shape=(
            jax.ShapeDtypeStruct((comps, nloc, chans), BF16),
            jax.ShapeDtypeStruct((comps, nloc, chans), F32),
            jax.ShapeDtypeStruct((LEVELS, chans, chans), F32),
            jax.ShapeDtypeStruct((LEVELS - 1, chans, chans), F32),
            jax.ShapeDtypeStruct((heads, chans), F32),
        ),
        in_specs=[vmem] * 4,
        out_specs=(hbm,) * 5,
        scratch_shapes=[dma((6,))],
        name="store",
    )(updated, node_grad, full, gate)
    return (updated.transpose(1, 0, 2), node_grad.transpose(1, 0, 2), real, imag, gate.T)


def solution(mesh):
    whole = P("dom", None, None)
    return jax.shard_map(
        shards,
        mesh=mesh,
        in_specs=(
            whole, whole, whole, P("dom", None), P("dom", None), P("dom", None), P("dom"), P(), P(), P(),
        ),
        out_specs=(whole, whole, P(), P(), P()),
        check_vma=False,
    )
```

```python
import functools

import jax
import jax.numpy as jnp
from jax import lax
from jax.experimental import pallas as pl
from jax.experimental.pallas import tpu as pltpu
from jax.sharding import PartitionSpec as P

MESH = pl.DeviceIdType.MESH
F32 = jnp.float32
BF16 = jnp.bfloat16
HIGHEST = lax.Precision.HIGHEST

LEVELS = 7
SLOT0 = [0, 4, 10, 15, 19, 22, 24, 25]
SLOTS = 25
CHUNKS = [(0, 4), (19, 6), (15, 4), (10, 5), (4, 6)]
CHUNK_ORDERS = [[0], [4, 5, 6], [3], [2], [1]]
E1 = (4, 3)
E2 = (2, 2)
LATE = (0, 2)
BATCHES = [E1, E2, LATE]


def dot(a, b, precision=None):
    return lax.dot_general(
        a, b, (((1,), (0,)), ((), ())), precision=precision, preferred_element_type=F32
    )


def dot_nt(a, b, precision=None):
    return lax.dot_general(
        a, b, (((1,), (1,)), ((), ())), precision=precision, preferred_element_type=F32
    )


def dot_tn(a, b, precision=None):
    return lax.dot_general(
        a, b, (((0,), (0,)), ((), ())), precision=precision, preferred_element_type=F32
    )


def iota(shape, dim):
    return lax.broadcasted_iota(jnp.int32, shape, dim)


def pair_comps(order, i):
    if order == 0:
        la = 2 * i + 1
        lb = 2 * i + 2
        return la * la + la, lb * lb + lb, 1 + i
    deg = i + order
    mid = deg * deg + deg
    return mid + order, mid - order, SLOT0[order] + i


def pair_count(order):
    return 3 if order == 0 else LEVELS - order


ALL_PAIRS = [(order, i) for order in range(LEVELS) for i in range(pair_count(order))]


def split(a, axis):
    high = a.astype(BF16)
    low = (a - high.astype(F32)).astype(BF16)
    return jnp.concatenate([high, low], axis=axis)


def remote(src, dst, send_sem, recv_sem, device):
    return pltpu.make_async_remote_copy(
        src_ref=src, dst_ref=dst, send_sem=send_sem, recv_sem=recv_sem,
        device_id=(device,), device_id_type=MESH,
    )


def main_kernel(
    nf_hbm, cot_hbm, bnd_hbm, src_hbm, dst_hbm, dist_hbm, cnt_hbm, wr_hbm, wi_hbm, wg_hbm,
    upd, ng, full, real0, gate,
    nf, cot, bnd_ref, src_ref, dst_ref, dist_ref, cnt_ref, wr_ref, wi_ref, wg_ref,
    pairs, vout, vin, vown, qout, table, pbuf, w256, xbuf, rcore, part, rxy, rz_own, rz,
    in_sem, vs_sem, vr_sem, qs_sem, qr_sem, core_sem, xs_sem, xr_sem, zs_sem, zr_sem, gs_sem, gr_sem,
):
    rounds = bnd_ref.shape[0]
    border = bnd_ref.shape[2]
    nloc = nf.shape[1]
    ghosts = rounds * border
    rows = nloc + ghosts
    edges = src_ref.shape[1]
    chans = nf.shape[2]
    heads = wg_ref.shape[0]
    width = chans // heads
    me = lax.axis_index("dom")
    core = me % 2
    xpos = (me // 2) % 4
    zpos = (me // 8) % 8
    ypos = me // 64
    plane = ypos * 4 + xpos
    half = chans
    tile = half // 16
    partners = [me + (1 << r) * (1 - 2 * ((me // (1 << r)) % 2)) for r in range(rounds)]
    other = partners[0]
    xy = [(plane + k) % 16 for k in range(16)]
    xy_from = [(plane + 16 - k) % 16 for k in range(16)]
    xy_device = [(j // 4) * 64 + zpos * 8 + (j % 4) * 2 + core for j in xy]
    z_from = [(zpos + 8 - k) % 8 for k in range(8)]
    z_slot = [zpos] * 8
    z_device = [ypos * 64 + ((zpos + k) % 8) * 8 + xpos * 2 + core for k in range(8)]

    sources = [cot_hbm, src_hbm, dst_hbm, dist_hbm, cnt_hbm, bnd_hbm, nf_hbm, wr_hbm, wi_hbm, wg_hbm]
    targets = [cot, src_ref, dst_ref, dist_ref, cnt_ref, bnd_ref, nf, wr_ref, wi_ref, wg_ref]
    loads = [
        pltpu.make_async_copy(a, b, in_sem.at[i]) for i, (a, b) in enumerate(zip(sources, targets))
    ]
    for load in loads:
        load.start()
    barrier = pltpu.get_barrier_semaphore()
    peers = [other] + xy_device[1:] + z_device[1:]
    for device in peers:
        pl.semaphore_signal(barrier, inc=1, device_id=(device,), device_id_type=MESH)

    for load in loads[1:5]:
        load.wait()
    live = (iota((1, edges), 1) < cnt_ref[0]).astype(F32)
    scale = (1.0 - dist_ref[...] / 5.0) ** 2 * live
    scaled = split(jnp.where(iota((rows, edges), 0) == src_ref[...], scale, 0.0), 0)
    into = (iota((nloc, edges), 0) == dst_ref[...]).astype(F32).astype(BF16)
    into2 = jnp.concatenate([into, into], axis=0)
    k2 = dot_nt(scaled, into2)
    k2 = 0.25 * (k2[:rows] + k2[rows:])
    high = k2.astype(BF16).astype(F32)
    k_mat = jnp.where(iota(k2.shape, 1) < nloc, high, k2 - high).astype(BF16)
    kt2 = dot_nt(into2, scaled[:rows]) + dot_nt(into2, scaled[rows:])
    kt2 = 0.25 * kt2
    high = kt2.astype(BF16).astype(F32)
    kt_mat = jnp.where(iota(kt2.shape, 0) < nloc, high, kt2 - high).astype(BF16)

    def v_halo(chunk, r):
        first, count = CHUNKS[chunk]
        at = (pl.ds(first, count), pl.ds(r * border, border), slice(None))
        return remote(vout.at[at], vin.at[at], vs_sem.at[chunk, r], vr_sem.at[chunk, r], partners[r])

    def q_halo(chunk, r):
        first, count = CHUNKS[chunk]
        return remote(
            qout.at[pl.ds(first, count), pl.ds(r * border, border), :],
            table.at[pl.ds(first, count), pl.ds(nloc + r * border, border), :],
            qs_sem.at[chunk, r], qr_sem.at[chunk, r], partners[r],
        )

    loads[0].wait()

    for chunk, orders in enumerate(CHUNK_ORDERS):
        if chunk == 0:
            v = dot(k_mat, jnp.concatenate([cot[0], cot[0]], axis=0))
            v = jnp.concatenate([v, jnp.zeros((rows, chans), F32)], axis=1)
            vown[0] = v[:nloc]
            vout[0] = v[nloc:].astype(BF16)
        for order in orders:
            for i in range(pair_count(order)):
                ca, cb, slot = pair_comps(order, i)
                both = jnp.concatenate([cot[ca], cot[cb]], axis=1)
                v = dot(k_mat, jnp.concatenate([both, both], axis=0))
                vown[slot] = v[:nloc]
                vout[slot] = v[nloc:].astype(BF16)
        if chunk == 0:
            pl.semaphore_wait(barrier, len(peers))
        for r in reversed(range(rounds)):
            v_halo(chunk, r).start()

    for load in loads[5:]:
        load.wait()
    bnd = bnd_ref[:, 0, :].astype(F32)
    tiled = dot(bnd, (iota((border, ghosts), 1) % border == iota((border, ghosts), 0)).astype(F32))
    own_round = iota((rounds, ghosts), 1) // border == iota((rounds, ghosts), 0)
    brow = jnp.sum(jnp.where(own_round, tiled, 0.0), axis=0, keepdims=True).astype(jnp.int32)
    bt = (iota((nloc, ghosts), 0) == brow).astype(F32).astype(BF16)
    eye = (iota((nloc, nloc), 0) == iota((nloc, nloc), 1)).astype(F32).astype(BF16)
    b = dot_tn(bt, eye).astype(BF16)

    zero_w = jnp.zeros((chans, chans), BF16)
    w256[0] = jnp.concatenate(
        [
            jnp.concatenate([wr_ref[0], zero_w], axis=1),
            jnp.concatenate([zero_w, wr_ref[0]], axis=1),
        ],
        axis=0,
    )
    for m in range(1, LEVELS):
        w256[m] = jnp.concatenate(
            [
                jnp.concatenate([wr_ref[m], wi_ref[m - 1]], axis=1),
                jnp.concatenate([-wi_ref[m - 1], wr_ref[m]], axis=1),
            ],
            axis=0,
        )
    head_of = iota((chans, heads), 0) // width == iota((chans, heads), 1)
    gate_rows = dot(head_of.astype(F32), wg_ref[...].astype(F32)).astype(BF16)

    p0 = dot(nf[0], wr_ref[0])
    att = jax.nn.sigmoid(dot_nt(split(p0, 1), jnp.concatenate([gate_rows, gate_rows], axis=1)))
    att2 = jnp.concatenate([att, att], axis=1)
    q = jnp.concatenate([att * p0, jnp.zeros((nloc, chans), F32)], axis=1).astype(BF16)
    table[0, pl.ds(0, nloc), :] = q
    qout[0] = dot(b, q).astype(BF16)
    for chunk, orders in enumerate(CHUNK_ORDERS):
        for order in orders:
            n = pair_count(order)
            first = pair_comps(order, 0)[2]
            for i in range(n):
                ca, cb, slot = pair_comps(order, i)
                pairs[slot] = jnp.concatenate([nf[ca], nf[cb]], axis=1)
            p = dot(pairs[pl.ds(first, n)].reshape(n * nloc, 2 * chans), w256[order])
            p = p.reshape(n, nloc, 2 * chans)
            pbuf[pl.ds(first, n)] = p
            for i in range(n):
                q = (att2 * p[i]).astype(BF16)
                table[first + i, pl.ds(0, nloc), :] = q
                qout[first + i] = dot(b, q).astype(BF16)

    def rows_of(core_half, j):
        return pl.ds(pl.multiple_of(core_half * half + j * tile, tile), tile)

    mine = pl.ds(pl.multiple_of(core * half, half), half)
    theirs = pl.ds(pl.multiple_of((1 - core) * half, half), half)

    def swap(batch):
        s = BATCHES.index(batch)
        at = pl.ds(*batch)
        return remote(xbuf.at[at, theirs, :], rcore.at[at], core_sem.at[s, 0], core_sem.at[s, 1], other)

    def scatter(batch, k):
        s = BATCHES.index(batch)
        at = pl.ds(*batch)
        own = pl.ds(pl.multiple_of(xy[k] * tile, tile), tile)
        return remote(part.at[at, own, :], rxy.at[k - 1, at], xs_sem.at[s], xr_sem.at[s], xy_device[k])

    def share(batch, k):
        s = BATCHES.index(batch)
        at = pl.ds(*batch)
        return remote(rz_own.at[at], rz.at[z_slot[k], at], zs_sem.at[s], zr_sem.at[s], z_device[k])

    def gather(batch, k):
        s = BATCHES.index(batch)
        ref = full.at[pl.ds(*batch), rows_of(core, plane), :]
        return remote(ref, ref, gs_sem.at[s], gr_sem.at[s], xy_device[k])

    def swap_back(batch, rows_half):
        s = BATCHES.index(batch)
        ref = full.at[pl.ds(*batch), rows_half, :]
        return remote(ref, ref, core_sem.at[s, 2], core_sem.at[s, 3], other)

    def all_scatter(batch):
        s = BATCHES.index(batch)
        ref = rxy.at[:, pl.ds(*batch)]
        return remote(ref, ref, xs_sem.at[s], xr_sem.at[s], other)

    def all_share(batch):
        s = BATCHES.index(batch)
        ref = rz.at[pl.ds(0, 7), pl.ds(*batch)]
        return remote(ref, ref, zs_sem.at[s], zr_sem.at[s], other)

    def all_gather(batch):
        s = BATCHES.index(batch)
        ref = rxy.at[:, pl.ds(*batch)]
        return remote(ref, ref, gs_sem.at[s], gr_sem.at[s], other)

    def after_swap(batch):
        swap(batch).wait_recv()
        at = pl.ds(*batch)
        part[at] = xbuf[at, mine, :] + rcore[at]
        for k in range(1, 16):
            scatter(batch, k).start()

    def after_scatter(batch):
        at = pl.ds(*batch)
        total = part[at, pl.ds(pl.multiple_of(plane * tile, tile), tile), :]
        all_scatter(batch).wait_recv()
        for k in range(1, 16):
            total += rxy[k - 1, at]
        rz_own[at] = total
        for k in range(1, 8):
            share(batch, k).start()

    def after_share(batch):
        at = pl.ds(*batch)
        all_share(batch).wait_recv()
        rz[zpos, at] = rz_own[at]
        total = rz[0, at]
        for k in range(1, 8):
            total += rz[k, at]
        full[at, rows_of(core, plane), :] = total
        for k in range(1, 16):
            gather(batch, k).start()

    def after_gather(batch):
        all_gather(batch).wait_recv()
        swap_back(batch, mine).start()

    def send_q(chunks, rounds_now):
        for chunk in chunks:
            for r in rounds_now:
                q_halo(chunk, r).start()

    v0 = None
    acc = None
    xbuf[0, pl.ds(chans, chans), :] = jnp.zeros((chans, chans), F32)
    for chunk, orders in enumerate(CHUNK_ORDERS):
        for r in range(rounds):
            v_halo(chunk, r).wait_recv()
        if chunk == 2:
            after_swap(E1)
        if chunk == 4:
            after_swap(E2)
        if chunk == 0:
            v0 = vown[0, :, pl.ds(0, chans)] + dot(bt, vin[0, :, pl.ds(0, chans)])
            acc = p0 * v0
        for order in orders:
            n = pair_count(order)
            first = pair_comps(order, 0)[2]
            z = []
            for i in range(n):
                v = vown[first + i] + dot(bt, vin[first + i])
                prod = pbuf[first + i] * v
                acc += prod[:, :chans] + prod[:, chans:]
                z.append(att2 * v)
            z = jnp.concatenate(z, axis=0)
            high = z.astype(BF16)
            low = (z - high.astype(F32)).astype(BF16)
            tc = dot_nt(high, w256[order]).reshape(n, nloc, 2 * chans)
            for i in range(n):
                ca, cb, slot = pair_comps(order, i)
                ng[ca] = cot[ca].astype(F32) + tc[i, :, :chans]
                ng[cb] = cot[cb].astype(F32) + tc[i, :, chans:]
            t = pairs[pl.ds(first, n)].reshape(n * nloc, 2 * chans)
            gw = dot_tn(jnp.concatenate([t, t], axis=0), jnp.concatenate([high, low], axis=0))
            real = gw[:chans, :chans] + gw[chans:, chans:]
            if order == 0:
                real += dot_tn(jnp.concatenate([nf[0], nf[0]], axis=0), split(att * v0, 0))
            else:
                xbuf[order, pl.ds(chans, chans), :] = gw[:chans, chans:] - gw[chans:, :chans]
            xbuf[order, pl.ds(0, chans), :] = real
        if chunk == 1:
            swap(E1).start()
        if chunk == 3:
            swap(E2).start()

    same_head = iota((chans, chans), 0) // width == iota((chans, chans), 1) // width
    same_head = same_head.astype(F32).astype(BF16)
    acc = dot(split(acc, 1), jnp.concatenate([same_head, same_head], axis=0))
    logit_cot = acc * att * (1.0 - att)
    lead = (iota((heads, chans), 1) == iota((heads, chans), 0) * width).astype(F32)
    outer = dot_tn(split(logit_cot, 0), jnp.concatenate([nf[0], nf[0]], axis=0))
    xbuf[0, pl.ds(chans, heads), :] = dot(lead, outer, HIGHEST)
    swap(LATE).start()

    def aggregate(q):
        u = dot(kt_mat, q)
        return u[:nloc] + u[nloc:]

    def forward(chunk):
        for r in range(rounds):
            q_halo(chunk, r).wait_recv()
        if chunk == 0:
            upd[0] = (nf[0].astype(F32) + aggregate(table[0, :, pl.ds(0, chans)])).astype(BF16)
        for order in CHUNK_ORDERS[chunk]:
            for i in range(pair_count(order)):
                ca, cb, slot = pair_comps(order, i)
                u = aggregate(table[slot])
                upd[ca] = (nf[ca].astype(F32) + u[:, :chans]).astype(BF16)
                upd[cb] = (nf[cb].astype(F32) + u[:, chans:]).astype(BF16)

    after_swap(LATE)
    lead_rows = jnp.where(iota((chans, chans), 0) % width == 0, gate_rows.astype(F32), 0.0).astype(BF16)
    z0 = att * v0 + dot(split(logit_cot, 1), jnp.concatenate([lead_rows, lead_rows], axis=0))
    ng[0] = cot[0].astype(F32) + dot_nt(z0.astype(BF16), wr_ref[0])
    after_scatter(E1)
    after_scatter(E2)
    after_scatter(LATE)
    after_share(E1)
    after_share(E2)
    after_share(LATE)
    send_q(range(5), [4, 3, 2, 1, 0])
    after_gather(E1)
    after_gather(E2)
    after_gather(LATE)
    forward(0)
    forward(1)
    forward(2)
    forward(3)
    forward(4)

    for batch in BATCHES:
        swap_back(batch, theirs).wait_recv()
    m_total = full[0, pl.ds(chans, heads), :]
    w0 = wr_ref[0]
    gate[...] = dot(split(m_total, 1), jnp.concatenate([w0, w0], axis=0))
    wg = wg_ref[...].astype(F32)
    late_real = dot_tn(split(m_total, 0), jnp.concatenate([wg, wg], axis=0).astype(BF16))
    real0[...] = full[0, pl.ds(0, chans), :] + late_real

    for chunk in range(len(CHUNKS)):
        for r in range(rounds):
            v_halo(chunk, r).wait_send()
            q_halo(chunk, r).wait_send()
    for batch in BATCHES:
        swap(batch).wait_send()
        all_scatter(batch).wait_send()
        all_share(batch).wait_send()
        all_gather(batch).wait_send()
        swap_back(batch, mine).wait_send()


def store_kernel(upd, ng, full, real0, gate, upd_hbm, ng_hbm, real_hbm, imag_hbm, gate_hbm, sem):
    chans = real_hbm.shape[1]
    above = pl.ds(1, LEVELS - 1)
    copies = [
        (ng, ng_hbm),
        (upd, upd_hbm),
        (full.at[above, pl.ds(0, chans), :], real_hbm.at[above]),
        (full.at[above, pl.ds(chans, chans), :], imag_hbm),
        (real0, real_hbm.at[0]),
        (gate, gate_hbm),
    ]
    copies = [pltpu.make_async_copy(a, b, sem.at[i]) for i, (a, b) in enumerate(copies)]
    for copy in copies:
        copy.start()
    for copy in copies:
        copy.wait()


def shards(
    node_feats, cotangent, boundary, edge_src, edge_dst, edge_dist, edge_count, w_real, w_imag, w_gate
):
    nloc, comps, chans = node_feats.shape
    rounds, border = boundary.shape[1:]
    heads = w_gate.shape[1]
    ghosts = rounds * border
    rows = nloc + ghosts
    chunks = len(CHUNKS)
    pair = 2 * chans
    tile = chans // 16
    vmem = pl.BlockSpec(memory_space=pltpu.VMEM)
    hbm = pl.BlockSpec(memory_space=pltpu.HBM)
    dma = pltpu.SemaphoreType.DMA
    inputs = (
        node_feats.transpose(1, 0, 2),
        cotangent.transpose(1, 0, 2),
        boundary.transpose(1, 0, 2),
        edge_src,
        edge_dst,
        edge_dist,
        edge_count,
        w_real,
        w_imag,
        w_gate.T,
    )
    inputs = [
        a if a.ndim == 1 else pltpu.with_memory_space_constraint(a, pltpu.HBM) for a in inputs
    ]
    held = [
        (pltpu.SMEM if i == 6 else pltpu.VMEM)(a.shape, a.dtype) for i, a in enumerate(inputs)
    ]
    updated, node_grad, full, real0, gate = pl.pallas_call(
        main_kernel,
        out_shape=(
            pltpu.VMEM((comps, nloc, chans), BF16),
            pltpu.VMEM((comps, nloc, chans), F32),
            pltpu.VMEM((LEVELS, pair, chans), F32),
            pltpu.VMEM((chans, chans), F32),
            pltpu.VMEM((heads, chans), F32),
        ),
        in_specs=[hbm] * len(inputs),
        out_specs=(vmem,) * 5,
        scratch_shapes=held + [
            pltpu.VMEM((SLOTS, nloc, pair), BF16),
            pltpu.VMEM((SLOTS, ghosts, pair), BF16),
            pltpu.VMEM((SLOTS, ghosts, pair), BF16),
            pltpu.VMEM((SLOTS, nloc, pair), F32),
            pltpu.VMEM((SLOTS, ghosts, pair), BF16),
            pltpu.VMEM((SLOTS, rows, pair), BF16),
            pltpu.VMEM((SLOTS, nloc, pair), F32),
            pltpu.VMEM((LEVELS, pair, pair), BF16),
            pltpu.VMEM((LEVELS, pair, chans), F32),
            pltpu.VMEM((LEVELS, chans, chans), F32),
            pltpu.VMEM((LEVELS, chans, chans), F32),
            pltpu.VMEM((15, LEVELS, tile, chans), F32),
            pltpu.VMEM((LEVELS, tile, chans), F32),
            pltpu.VMEM((8, LEVELS, tile, chans), F32),
            dma((len(inputs),)),
            dma((chunks, rounds)),
            dma((chunks, rounds)),
            dma((chunks, rounds)),
            dma((chunks, rounds)),
            dma((len(BATCHES), 4)),
            dma((len(BATCHES),)),
            dma((len(BATCHES),)),
            dma((len(BATCHES),)),
            dma((len(BATCHES),)),
            dma((len(BATCHES),)),
            dma((len(BATCHES),)),
        ],
        compiler_params=pltpu.CompilerParams(
            collective_id=0, has_side_effects=True, vmem_limit_bytes=40 * 2**20
        ),
        name="halo_edges",
    )(*inputs)
    updated, node_grad, real, imag, gate = pl.pallas_call(
        store_kernel,
        out_shape=(
            jax.ShapeDtypeStruct((comps, nloc, chans), BF16),
            jax.ShapeDtypeStruct((comps, nloc, chans), F32),
            jax.ShapeDtypeStruct((LEVELS, chans, chans), F32),
            jax.ShapeDtypeStruct((LEVELS - 1, chans, chans), F32),
            jax.ShapeDtypeStruct((heads, chans), F32),
        ),
        in_specs=[vmem] * 5,
        out_specs=(hbm,) * 5,
        scratch_shapes=[dma((6,))],
        compiler_params=pltpu.CompilerParams(vmem_limit_bytes=2 * 2**20),
        name="store",
    )(updated, node_grad, full, real0, gate)
    return (updated.transpose(1, 0, 2), node_grad.transpose(1, 0, 2), real, imag, gate.T)


def solution(mesh):
    whole = P("dom", None, None)
    return jax.shard_map(
        shards,
        mesh=mesh,
        in_specs=(
            whole, whole, whole, P("dom", None), P("dom", None), P("dom", None), P("dom"), P(), P(), P(),
        ),
        out_specs=(whole, whole, P(), P(), P()),
        check_vma=False,
    )
```

```python
import functools

import jax
import jax.numpy as jnp
from jax import lax
from jax.experimental import pallas as pl
from jax.experimental.pallas import tpu as pltpu
from jax.sharding import PartitionSpec as P

MESH = pl.DeviceIdType.MESH
F32 = jnp.float32
BF16 = jnp.bfloat16
HIGHEST = lax.Precision.HIGHEST

LEVELS = 7
SLOT0 = [0, 4, 10, 15, 19, 22, 24, 25]
SLOTS = 25
CHUNKS = [(0, 4), (19, 6), (15, 4), (10, 5), (4, 6)]
CHUNK_ORDERS = [[0], [4, 5, 6], [3], [2], [1]]
E1 = (4, 3)
E2 = (2, 2)
LATE = (0, 2)
BATCHES = [E1, E2, LATE]


def dot(a, b, precision=None):
    return lax.dot_general(
        a, b, (((1,), (0,)), ((), ())), precision=precision, preferred_element_type=F32
    )


def dot_nt(a, b, precision=None):
    return lax.dot_general(
        a, b, (((1,), (1,)), ((), ())), precision=precision, preferred_element_type=F32
    )


def dot_tn(a, b, precision=None):
    return lax.dot_general(
        a, b, (((0,), (0,)), ((), ())), precision=precision, preferred_element_type=F32
    )


def iota(shape, dim):
    return lax.broadcasted_iota(jnp.int32, shape, dim)


def pair_comps(order, i):
    if order == 0:
        la = 2 * i + 1
        lb = 2 * i + 2
        return la * la + la, lb * lb + lb, 1 + i
    deg = i + order
    mid = deg * deg + deg
    return mid + order, mid - order, SLOT0[order] + i


def pair_count(order):
    return 3 if order == 0 else LEVELS - order


ALL_PAIRS = [(order, i) for order in range(LEVELS) for i in range(pair_count(order))]


def split(a, axis):
    high = a.astype(BF16)
    low = (a - high.astype(F32)).astype(BF16)
    return jnp.concatenate([high, low], axis=axis)


def remote(src, dst, send_sem, recv_sem, device):
    return pltpu.make_async_remote_copy(
        src_ref=src, dst_ref=dst, send_sem=send_sem, recv_sem=recv_sem,
        device_id=(device,), device_id_type=MESH,
    )


def main_kernel(
    nf_hbm, cot_hbm, bnd_hbm, src_hbm, dst_hbm, dist_hbm, cnt_hbm, wr_hbm, wi_hbm, wg_hbm,
    upd, ng, full, real0, gate,
    nf, cot, bnd_ref, src_ref, dst_ref, dist_ref, cnt_ref, wr_ref, wi_ref, wg_ref,
    pairs, vout, vin, vown, qout, table, pbuf, w256, xbuf, rcore, part, rxy, rz_own, rz, gathered0, gathered1, gathered2,
    in_sem, vs_sem, vr_sem, qs_sem, qr_sem, core_sem, xs_sem, xr_sem, zs_sem, zr_sem, gs_sem, gr_sem,
):
    gathered = [gathered0, gathered1, gathered2]
    rounds = bnd_ref.shape[0]
    border = bnd_ref.shape[2]
    nloc = nf.shape[1]
    ghosts = rounds * border
    rows = nloc + ghosts
    edges = src_ref.shape[1]
    chans = nf.shape[2]
    heads = wg_ref.shape[0]
    width = chans // heads
    me = lax.axis_index("dom")
    core = me % 2
    xpos = (me // 2) % 4
    zpos = (me // 8) % 8
    ypos = me // 64
    plane = ypos * 4 + xpos
    half = chans
    tile = half // 16
    partners = [me + (1 << r) * (1 - 2 * ((me // (1 << r)) % 2)) for r in range(rounds)]
    other = partners[0]
    xy = [(plane + k) % 16 for k in range(16)]
    xy_from = [(plane + 16 - k) % 16 for k in range(16)]
    xy_device = [(j // 4) * 64 + zpos * 8 + (j % 4) * 2 + core for j in xy]
    z_from = [(zpos + 8 - k) % 8 for k in range(8)]
    z_slot = [zpos] * 8
    z_device = [ypos * 64 + ((zpos + k) % 8) * 8 + xpos * 2 + core for k in range(8)]

    sources = [cot_hbm, src_hbm, dst_hbm, dist_hbm, cnt_hbm, bnd_hbm, nf_hbm, wr_hbm, wi_hbm, wg_hbm]
    targets = [cot, src_ref, dst_ref, dist_ref, cnt_ref, bnd_ref, nf, wr_ref, wi_ref, wg_ref]
    loads = [
        pltpu.make_async_copy(a, b, in_sem.at[i]) for i, (a, b) in enumerate(zip(sources, targets))
    ]
    for load in loads:
        load.start()
    barrier = pltpu.get_barrier_semaphore()
    peers = [other] + xy_device[1:] + z_device[1:]
    for device in peers:
        pl.semaphore_signal(barrier, inc=1, device_id=(device,), device_id_type=MESH)

    for load in loads[1:5]:
        load.wait()
    live = (iota((1, edges), 1) < cnt_ref[0]).astype(F32)
    scale = (1.0 - dist_ref[...] / 5.0) ** 2 * live
    scaled = split(jnp.where(iota((rows, edges), 0) == src_ref[...], scale, 0.0), 0)
    into = (iota((nloc, edges), 0) == dst_ref[...]).astype(F32).astype(BF16)
    into2 = jnp.concatenate([into, into], axis=0)
    k2 = dot_nt(scaled, into2)
    k2 = 0.25 * (k2[:rows] + k2[rows:])
    high = k2.astype(BF16).astype(F32)
    k_mat = jnp.where(iota(k2.shape, 1) < nloc, high, k2 - high).astype(BF16)
    kt2 = dot_nt(into2, scaled[:rows]) + dot_nt(into2, scaled[rows:])
    kt2 = 0.25 * kt2
    high = kt2.astype(BF16).astype(F32)
    kt_mat = jnp.where(iota(kt2.shape, 0) < nloc, high, kt2 - high).astype(BF16)

    def v_halo(chunk, r):
        first, count = CHUNKS[chunk]
        at = (pl.ds(first, count), pl.ds(r * border, border), slice(None))
        return remote(vout.at[at], vin.at[at], vs_sem.at[chunk, r], vr_sem.at[chunk, r], partners[r])

    def q_halo(chunk, r):
        first, count = CHUNKS[chunk]
        return remote(
            qout.at[pl.ds(first, count), pl.ds(r * border, border), :],
            table.at[pl.ds(first, count), pl.ds(nloc + r * border, border), :],
            qs_sem.at[chunk, r], qr_sem.at[chunk, r], partners[r],
        )

    loads[0].wait()

    for chunk, orders in enumerate(CHUNK_ORDERS):
        if chunk == 0:
            v = dot(k_mat, jnp.concatenate([cot[0], cot[0]], axis=0))
            v = jnp.concatenate([v, jnp.zeros((rows, chans), F32)], axis=1)
            vown[0] = v[:nloc]
            vout[0] = v[nloc:].astype(BF16)
        for order in orders:
            for i in range(pair_count(order)):
                ca, cb, slot = pair_comps(order, i)
                both = jnp.concatenate([cot[ca], cot[cb]], axis=1)
                v = dot(k_mat, jnp.concatenate([both, both], axis=0))
                vown[slot] = v[:nloc]
                vout[slot] = v[nloc:].astype(BF16)
        if chunk == 0:
            pl.semaphore_wait(barrier, len(peers))
        for r in reversed(range(rounds)):
            v_halo(chunk, r).start()

    for load in loads[5:]:
        load.wait()
    bnd = bnd_ref[:, 0, :].astype(F32)
    tiled = dot(bnd, (iota((border, ghosts), 1) % border == iota((border, ghosts), 0)).astype(F32))
    own_round = iota((rounds, ghosts), 1) // border == iota((rounds, ghosts), 0)
    brow = jnp.sum(jnp.where(own_round, tiled, 0.0), axis=0, keepdims=True).astype(jnp.int32)
    bt = (iota((nloc, ghosts), 0) == brow).astype(F32).astype(BF16)
    eye = (iota((nloc, nloc), 0) == iota((nloc, nloc), 1)).astype(F32).astype(BF16)
    b = dot_tn(bt, eye).astype(BF16)

    zero_w = jnp.zeros((chans, chans), BF16)
    w256[0] = jnp.concatenate(
        [
            jnp.concatenate([wr_ref[0], zero_w], axis=1),
            jnp.concatenate([zero_w, wr_ref[0]], axis=1),
        ],
        axis=0,
    )
    for m in range(1, LEVELS):
        w256[m] = jnp.concatenate(
            [
                jnp.concatenate([wr_ref[m], wi_ref[m - 1]], axis=1),
                jnp.concatenate([-wi_ref[m - 1], wr_ref[m]], axis=1),
            ],
            axis=0,
        )
    head_of = iota((chans, heads), 0) // width == iota((chans, heads), 1)
    gate_rows = dot(head_of.astype(F32), wg_ref[...].astype(F32)).astype(BF16)

    p0 = dot(nf[0], wr_ref[0])
    att = jax.nn.sigmoid(dot_nt(split(p0, 1), jnp.concatenate([gate_rows, gate_rows], axis=1)))
    att2 = jnp.concatenate([att, att], axis=1)
    q = jnp.concatenate([att * p0, jnp.zeros((nloc, chans), F32)], axis=1).astype(BF16)
    table[0, pl.ds(0, nloc), :] = q
    qout[0] = dot(b, q).astype(BF16)
    for chunk, orders in enumerate(CHUNK_ORDERS):
        for order in orders:
            n = pair_count(order)
            first = pair_comps(order, 0)[2]
            for i in range(n):
                ca, cb, slot = pair_comps(order, i)
                pairs[slot] = jnp.concatenate([nf[ca], nf[cb]], axis=1)
            p = dot(pairs[pl.ds(first, n)].reshape(n * nloc, 2 * chans), w256[order])
            p = p.reshape(n, nloc, 2 * chans)
            pbuf[pl.ds(first, n)] = p
            for i in range(n):
                q = (att2 * p[i]).astype(BF16)
                table[first + i, pl.ds(0, nloc), :] = q
                qout[first + i] = dot(b, q).astype(BF16)

    mine = pl.ds(pl.multiple_of(core * half, half), half)
    theirs = pl.ds(pl.multiple_of((1 - core) * half, half), half)

    def swap(batch):
        s = BATCHES.index(batch)
        at = pl.ds(*batch)
        return remote(xbuf.at[at, theirs, :], rcore.at[at], core_sem.at[s, 0], core_sem.at[s, 1], other)

    def scatter(batch, k):
        s = BATCHES.index(batch)
        at = pl.ds(*batch)
        own = pl.ds(pl.multiple_of(xy[k] * tile, tile), tile)
        return remote(part.at[at, own, :], rxy.at[k - 1, at], xs_sem.at[s], xr_sem.at[s], xy_device[k])

    def share(batch, k):
        s = BATCHES.index(batch)
        at = pl.ds(*batch)
        return remote(rz_own.at[at], rz.at[z_slot[k], at], zs_sem.at[s], zr_sem.at[s], z_device[k])

    def gather(batch, k):
        s = BATCHES.index(batch)
        ref = gathered[s].at[core, plane]
        return remote(ref, ref, gs_sem.at[s], gr_sem.at[s], xy_device[k])

    def swap_back(batch, core_half):
        s = BATCHES.index(batch)
        ref = gathered[s].at[core_half]
        return remote(ref, ref, core_sem.at[s, 2], core_sem.at[s, 3], other)

    def all_scatter(batch):
        s = BATCHES.index(batch)
        ref = rxy.at[:, pl.ds(*batch)]
        return remote(ref, ref, xs_sem.at[s], xr_sem.at[s], other)

    def all_share(batch):
        s = BATCHES.index(batch)
        ref = rz.at[pl.ds(0, 7), pl.ds(*batch)]
        return remote(ref, ref, zs_sem.at[s], zr_sem.at[s], other)

    def all_gather(batch):
        s = BATCHES.index(batch)
        ref = gathered[s].at[core, pl.ds(0, 15)]
        return remote(ref, ref, gs_sem.at[s], gr_sem.at[s], other)

    def after_swap(batch):
        swap(batch).wait_recv()
        at = pl.ds(*batch)
        part[at] = xbuf[at, mine, :] + rcore[at]
        for k in range(1, 16):
            scatter(batch, k).start()

    def after_scatter(batch):
        at = pl.ds(*batch)
        total = part[at, pl.ds(pl.multiple_of(plane * tile, tile), tile), :]
        all_scatter(batch).wait_recv()
        for k in range(1, 16):
            total += rxy[k - 1, at]
        rz_own[at] = total
        for k in range(1, 8):
            share(batch, k).start()

    def after_share(batch):
        at = pl.ds(*batch)
        all_share(batch).wait_recv()
        rz[zpos, at] = rz_own[at]
        total = rz[0, at]
        for k in range(1, 8):
            total += rz[k, at]
        total = total.reshape(batch[1] * tile, chans)
        ref = gathered[BATCHES.index(batch)]
        if ref.shape[2] > total.shape[0]:
            spare = jnp.zeros((ref.shape[2] - total.shape[0], chans), F32)
            total = jnp.concatenate([total, spare], axis=0)
        ref[core, plane] = total.astype(BF16)
        for k in range(1, 16):
            gather(batch, k).start()

    def after_gather(batch):
        all_gather(batch).wait_recv()
        swap_back(batch, core).start()

    def unpack(batch):
        first, n = batch
        swap_back(batch, 1 - core).wait_recv()
        ref = gathered[BATCHES.index(batch)]
        for half_index in range(2):
            for j in range(16):
                t = ref[half_index, j].astype(F32)[: n * tile].reshape(n, tile, chans)
                full[pl.ds(first, n), pl.ds(half_index * half + j * tile, tile), :] = t

    def send_q(chunks, rounds_now):
        for chunk in chunks:
            for r in rounds_now:
                q_halo(chunk, r).start()

    v0 = None
    acc = None
    xbuf[0, pl.ds(chans, chans), :] = jnp.zeros((chans, chans), F32)
    for chunk, orders in enumerate(CHUNK_ORDERS):
        for r in range(rounds):
            v_halo(chunk, r).wait_recv()
        if chunk == 2:
            after_swap(E1)
        if chunk == 4:
            after_swap(E2)
        if chunk == 0:
            v0 = vown[0, :, pl.ds(0, chans)] + dot(bt, vin[0, :, pl.ds(0, chans)])
            acc = p0 * v0
        for order in orders:
            n = pair_count(order)
            first = pair_comps(order, 0)[2]
            z = []
            for i in range(n):
                v = vown[first + i] + dot(bt, vin[first + i])
                prod = pbuf[first + i] * v
                acc += prod[:, :chans] + prod[:, chans:]
                z.append(att2 * v)
            z = jnp.concatenate(z, axis=0)
            high = z.astype(BF16)
            low = (z - high.astype(F32)).astype(BF16)
            tc = dot_nt(high, w256[order]).reshape(n, nloc, 2 * chans)
            for i in range(n):
                ca, cb, slot = pair_comps(order, i)
                ng[ca] = cot[ca].astype(F32) + tc[i, :, :chans]
                ng[cb] = cot[cb].astype(F32) + tc[i, :, chans:]
            t = pairs[pl.ds(first, n)].reshape(n * nloc, 2 * chans)
            gw = dot_tn(jnp.concatenate([t, t], axis=0), jnp.concatenate([high, low], axis=0))
            real = gw[:chans, :chans] + gw[chans:, chans:]
            if order == 0:
                real += dot_tn(jnp.concatenate([nf[0], nf[0]], axis=0), split(att * v0, 0))
            else:
                xbuf[order, pl.ds(chans, chans), :] = gw[:chans, chans:] - gw[chans:, :chans]
            xbuf[order, pl.ds(0, chans), :] = real
        if chunk == 1:
            swap(E1).start()
        if chunk == 3:
            swap(E2).start()

    same_head = iota((chans, chans), 0) // width == iota((chans, chans), 1) // width
    same_head = same_head.astype(F32).astype(BF16)
    acc = dot(split(acc, 1), jnp.concatenate([same_head, same_head], axis=0))
    logit_cot = acc * att * (1.0 - att)
    lead = (iota((heads, chans), 1) == iota((heads, chans), 0) * width).astype(F32)
    outer = dot_tn(split(logit_cot, 0), jnp.concatenate([nf[0], nf[0]], axis=0))
    xbuf[0, pl.ds(chans, heads), :] = dot(lead, outer, HIGHEST)
    swap(LATE).start()

    def aggregate(q):
        u = dot(kt_mat, q)
        return u[:nloc] + u[nloc:]

    def forward(chunk):
        for r in range(rounds):
            q_halo(chunk, r).wait_recv()
        if chunk == 0:
            upd[0] = (nf[0].astype(F32) + aggregate(table[0, :, pl.ds(0, chans)])).astype(BF16)
        for order in CHUNK_ORDERS[chunk]:
            for i in range(pair_count(order)):
                ca, cb, slot = pair_comps(order, i)
                u = aggregate(table[slot])
                upd[ca] = (nf[ca].astype(F32) + u[:, :chans]).astype(BF16)
                upd[cb] = (nf[cb].astype(F32) + u[:, chans:]).astype(BF16)

    after_swap(LATE)
    send_q([0], [4, 3, 2, 1, 0])
    lead_rows = jnp.where(iota((chans, chans), 0) % width == 0, gate_rows.astype(F32), 0.0).astype(BF16)
    z0 = att * v0 + dot(split(logit_cot, 1), jnp.concatenate([lead_rows, lead_rows], axis=0))
    ng[0] = cot[0].astype(F32) + dot_nt(z0.astype(BF16), wr_ref[0])
    after_scatter(E1)
    after_scatter(E2)
    after_scatter(LATE)
    send_q([1, 2], [4, 3, 2, 1, 0])
    after_share(E1)
    after_share(E2)
    after_share(LATE)
    send_q([3, 4], [4, 3, 2, 1, 0])
    after_gather(E1)
    after_gather(E2)
    unpack(E1)
    unpack(E2)
    after_gather(LATE)
    forward(0)
    forward(1)
    forward(2)
    forward(3)
    forward(4)
    unpack(LATE)

    m_total = full[0, pl.ds(chans, heads), :]
    w0 = wr_ref[0]
    gate[...] = dot(split(m_total, 1), jnp.concatenate([w0, w0], axis=0))
    wg = wg_ref[...].astype(F32)
    late_real = dot_tn(split(m_total, 0), jnp.concatenate([wg, wg], axis=0).astype(BF16))
    real0[...] = full[0, pl.ds(0, chans), :] + late_real

    for chunk in range(len(CHUNKS)):
        for r in range(rounds):
            v_halo(chunk, r).wait_send()
            q_halo(chunk, r).wait_send()
    for batch in BATCHES:
        swap(batch).wait_send()
        all_scatter(batch).wait_send()
        all_share(batch).wait_send()
        all_gather(batch).wait_send()
        swap_back(batch, core).wait_send()


def store_kernel(upd, ng, full, real0, gate, upd_hbm, ng_hbm, real_hbm, imag_hbm, gate_hbm, sem):
    chans = real_hbm.shape[1]
    above = pl.ds(1, LEVELS - 1)
    copies = [
        (ng, ng_hbm),
        (upd, upd_hbm),
        (full.at[above, pl.ds(0, chans), :], real_hbm.at[above]),
        (full.at[above, pl.ds(chans, chans), :], imag_hbm),
        (real0, real_hbm.at[0]),
        (gate, gate_hbm),
    ]
    copies = [pltpu.make_async_copy(a, b, sem.at[i]) for i, (a, b) in enumerate(copies)]
    for copy in copies:
        copy.start()
    for copy in copies:
        copy.wait()


def shards(
    node_feats, cotangent, boundary, edge_src, edge_dst, edge_dist, edge_count, w_real, w_imag, w_gate
):
    nloc, comps, chans = node_feats.shape
    rounds, border = boundary.shape[1:]
    heads = w_gate.shape[1]
    ghosts = rounds * border
    rows = nloc + ghosts
    chunks = len(CHUNKS)
    pair = 2 * chans
    tile = chans // 16
    vmem = pl.BlockSpec(memory_space=pltpu.VMEM)
    hbm = pl.BlockSpec(memory_space=pltpu.HBM)
    dma = pltpu.SemaphoreType.DMA
    inputs = (
        node_feats.transpose(1, 0, 2),
        cotangent.transpose(1, 0, 2),
        boundary.transpose(1, 0, 2),
        edge_src,
        edge_dst,
        edge_dist,
        edge_count,
        w_real,
        w_imag,
        w_gate.T,
    )
    inputs = [
        a if a.ndim == 1 else pltpu.with_memory_space_constraint(a, pltpu.HBM) for a in inputs
    ]
    held = [
        (pltpu.SMEM if i == 6 else pltpu.VMEM)(a.shape, a.dtype) for i, a in enumerate(inputs)
    ]
    updated, node_grad, full, real0, gate = pl.pallas_call(
        main_kernel,
        out_shape=(
            pltpu.VMEM((comps, nloc, chans), BF16),
            pltpu.VMEM((comps, nloc, chans), F32),
            pltpu.VMEM((LEVELS, pair, chans), F32),
            pltpu.VMEM((chans, chans), F32),
            pltpu.VMEM((heads, chans), F32),
        ),
        in_specs=[hbm] * len(inputs),
        out_specs=(vmem,) * 5,
        scratch_shapes=held + [
            pltpu.VMEM((SLOTS, nloc, pair), BF16),
            pltpu.VMEM((SLOTS, ghosts, pair), BF16),
            pltpu.VMEM((SLOTS, ghosts, pair), BF16),
            pltpu.VMEM((SLOTS, nloc, pair), F32),
            pltpu.VMEM((SLOTS, ghosts, pair), BF16),
            pltpu.VMEM((SLOTS, rows, pair), BF16),
            pltpu.VMEM((SLOTS, nloc, pair), F32),
            pltpu.VMEM((LEVELS, pair, pair), BF16),
            pltpu.VMEM((LEVELS, pair, chans), F32),
            pltpu.VMEM((LEVELS, chans, chans), F32),
            pltpu.VMEM((LEVELS, chans, chans), F32),
            pltpu.VMEM((15, LEVELS, tile, chans), F32),
            pltpu.VMEM((LEVELS, tile, chans), F32),
            pltpu.VMEM((8, LEVELS, tile, chans), F32),
        ] + [
            pltpu.VMEM((2, 16, -(-n * tile // 16) * 16, chans), BF16) for _, n in BATCHES
        ] + [
            dma((len(inputs),)),
            dma((chunks, rounds)),
            dma((chunks, rounds)),
            dma((chunks, rounds)),
            dma((chunks, rounds)),
            dma((len(BATCHES), 4)),
            dma((len(BATCHES),)),
            dma((len(BATCHES),)),
            dma((len(BATCHES),)),
            dma((len(BATCHES),)),
            dma((len(BATCHES),)),
            dma((len(BATCHES),)),
        ],
        compiler_params=pltpu.CompilerParams(
            collective_id=0, has_side_effects=True, vmem_limit_bytes=40 * 2**20
        ),
        name="halo_edges",
    )(*inputs)
    updated, node_grad, real, imag, gate = pl.pallas_call(
        store_kernel,
        out_shape=(
            jax.ShapeDtypeStruct((comps, nloc, chans), BF16),
            jax.ShapeDtypeStruct((comps, nloc, chans), F32),
            jax.ShapeDtypeStruct((LEVELS, chans, chans), F32),
            jax.ShapeDtypeStruct((LEVELS - 1, chans, chans), F32),
            jax.ShapeDtypeStruct((heads, chans), F32),
        ),
        in_specs=[vmem] * 5,
        out_specs=(hbm,) * 5,
        scratch_shapes=[dma((6,))],
        compiler_params=pltpu.CompilerParams(vmem_limit_bytes=2 * 2**20),
        name="store",
    )(updated, node_grad, full, real0, gate)
    return (updated.transpose(1, 0, 2), node_grad.transpose(1, 0, 2), real, imag, gate.T)


def solution(mesh):
    whole = P("dom", None, None)
    return jax.shard_map(
        shards,
        mesh=mesh,
        in_specs=(
            whole, whole, whole, P("dom", None), P("dom", None), P("dom", None), P("dom"), P(), P(), P(),
        ),
        out_specs=(whole, whole, P(), P(), P()),
        check_vma=False,
    )
```

```python
import functools

import jax
import jax.numpy as jnp
from jax import lax
from jax.experimental import pallas as pl
from jax.experimental.pallas import tpu as pltpu
from jax.sharding import PartitionSpec as P

MESH = pl.DeviceIdType.MESH
F32 = jnp.float32
BF16 = jnp.bfloat16
HIGHEST = lax.Precision.HIGHEST

LEVELS = 7
SLOT0 = [0, 4, 10, 15, 19, 22, 24, 25]
SLOTS = 25
CHUNKS = [(0, 4), (19, 6), (15, 4), (10, 5), (4, 6)]
CHUNK_ORDERS = [[0], [4, 5, 6], [3], [2], [1]]
E1 = (4, 3)
E2 = (2, 2)
LATE = (0, 2)
BATCHES = [E1, E2, LATE]
XY_FAR_FIRST = sorted(range(1, 16), key=lambda k: -(min(k % 4, 4 - k % 4) + min(k // 4, 4 - k // 4)))
Z_FAR_FIRST = [4, 3, 5, 2, 6, 1, 7]


def dot(a, b, precision=None):
    return lax.dot_general(
        a, b, (((1,), (0,)), ((), ())), precision=precision, preferred_element_type=F32
    )


def dot_nt(a, b, precision=None):
    return lax.dot_general(
        a, b, (((1,), (1,)), ((), ())), precision=precision, preferred_element_type=F32
    )


def dot_tn(a, b, precision=None):
    return lax.dot_general(
        a, b, (((0,), (0,)), ((), ())), precision=precision, preferred_element_type=F32
    )


def iota(shape, dim):
    return lax.broadcasted_iota(jnp.int32, shape, dim)


def pair_comps(order, i):
    if order == 0:
        la = 2 * i + 1
        lb = 2 * i + 2
        return la * la + la, lb * lb + lb, 1 + i
    deg = i + order
    mid = deg * deg + deg
    return mid + order, mid - order, SLOT0[order] + i


def pair_count(order):
    return 3 if order == 0 else LEVELS - order


ALL_PAIRS = [(order, i) for order in range(LEVELS) for i in range(pair_count(order))]


def split(a, axis):
    high = a.astype(BF16)
    low = (a - high.astype(F32)).astype(BF16)
    return jnp.concatenate([high, low], axis=axis)


def remote(src, dst, send_sem, recv_sem, device):
    return pltpu.make_async_remote_copy(
        src_ref=src, dst_ref=dst, send_sem=send_sem, recv_sem=recv_sem,
        device_id=(device,), device_id_type=MESH,
    )


def main_kernel(
    nf_hbm, cot_hbm, bnd_hbm, src_hbm, dst_hbm, dist_hbm, cnt_hbm, wr_hbm, wi_hbm, wg_hbm,
    upd, ng, full, real0, gate,
    nf, cot, bnd_ref, src_ref, dst_ref, dist_ref, cnt_ref, wr_ref, wi_ref, wg_ref,
    pairs, vout, vin, vown, qout, table, pbuf, w256, xbuf, rcore, part, rxy, rz_own, rz, gathered0, gathered1, gathered2,
    in_sem, vs_sem, vr_sem, qs_sem, qr_sem, core_sem, xs_sem, xr_sem, zs_sem, zr_sem, gs_sem, gr_sem,
):
    gathered = [gathered0, gathered1, gathered2]
    rounds = bnd_ref.shape[0]
    border = bnd_ref.shape[2]
    nloc = nf.shape[1]
    ghosts = rounds * border
    rows = nloc + ghosts
    edges = src_ref.shape[1]
    chans = nf.shape[2]
    heads = wg_ref.shape[0]
    width = chans // heads
    me = lax.axis_index("dom")
    core = me % 2
    xpos = (me // 2) % 4
    zpos = (me // 8) % 8
    ypos = me // 64
    plane = ypos * 4 + xpos
    half = chans
    tile = half // 16
    partners = [me + (1 << r) * (1 - 2 * ((me // (1 << r)) % 2)) for r in range(rounds)]
    other = partners[0]
    xy = [((ypos + k // 4) % 4) * 4 + (xpos + k % 4) % 4 for k in range(16)]
    xy_device = [(j // 4) * 64 + zpos * 8 + (j % 4) * 2 + core for j in xy]
    z_from = [(zpos + 8 - k) % 8 for k in range(8)]
    z_slot = [zpos] * 8
    z_device = [ypos * 64 + ((zpos + k) % 8) * 8 + xpos * 2 + core for k in range(8)]

    sources = [cot_hbm, src_hbm, dst_hbm, dist_hbm, cnt_hbm, bnd_hbm, nf_hbm, wr_hbm, wi_hbm, wg_hbm]
    targets = [cot, src_ref, dst_ref, dist_ref, cnt_ref, bnd_ref, nf, wr_ref, wi_ref, wg_ref]
    loads = [
        pltpu.make_async_copy(a, b, in_sem.at[i]) for i, (a, b) in enumerate(zip(sources, targets))
    ]
    for load in loads:
        load.start()
    barrier = pltpu.get_barrier_semaphore()
    peers = [other] + xy_device[1:] + z_device[1:]
    for device in peers:
        pl.semaphore_signal(barrier, inc=1, device_id=(device,), device_id_type=MESH)

    for load in loads[1:5]:
        load.wait()
    live = (iota((1, edges), 1) < cnt_ref[0]).astype(F32)
    scale = (1.0 - dist_ref[...] / 5.0) ** 2 * live
    scaled = split(jnp.where(iota((rows, edges), 0) == src_ref[...], scale, 0.0), 0)
    into = (iota((nloc, edges), 0) == dst_ref[...]).astype(F32).astype(BF16)
    into2 = jnp.concatenate([into, into], axis=0)
    k2 = dot_nt(scaled, into2)
    k2 = 0.25 * (k2[:rows] + k2[rows:])
    high = k2.astype(BF16).astype(F32)
    k_mat = jnp.where(iota(k2.shape, 1) < nloc, high, k2 - high).astype(BF16)
    kt2 = dot_nt(into2, scaled[:rows]) + dot_nt(into2, scaled[rows:])
    kt2 = 0.25 * kt2
    high = kt2.astype(BF16).astype(F32)
    kt_mat = jnp.where(iota(kt2.shape, 0) < nloc, high, kt2 - high).astype(BF16)

    def v_halo(chunk, r):
        first, count = CHUNKS[chunk]
        at = (pl.ds(first, count), pl.ds(r * border, border), slice(None))
        return remote(vout.at[at], vin.at[at], vs_sem.at[chunk, r], vr_sem.at[chunk, r], partners[r])

    def q_halo(chunk, r):
        first, count = CHUNKS[chunk]
        return remote(
            qout.at[pl.ds(first, count), pl.ds(r * border, border), :],
            table.at[pl.ds(first, count), pl.ds(nloc + r * border, border), :],
            qs_sem.at[chunk, r], qr_sem.at[chunk, r], partners[r],
        )

    loads[0].wait()

    for chunk, orders in enumerate(CHUNK_ORDERS):
        if chunk == 0:
            v = dot(k_mat, jnp.concatenate([cot[0], cot[0]], axis=0))
            v = jnp.concatenate([v, jnp.zeros((rows, chans), F32)], axis=1)
            vown[0] = v[:nloc]
            vout[0] = v[nloc:].astype(BF16)
        for order in orders:
            for i in range(pair_count(order)):
                ca, cb, slot = pair_comps(order, i)
                both = jnp.concatenate([cot[ca], cot[cb]], axis=1)
                v = dot(k_mat, jnp.concatenate([both, both], axis=0))
                vown[slot] = v[:nloc]
                vout[slot] = v[nloc:].astype(BF16)
        if chunk == 0:
            pl.semaphore_wait(barrier, len(peers))
        for r in reversed(range(rounds)):
            v_halo(chunk, r).start()

    for load in loads[5:]:
        load.wait()
    bnd = bnd_ref[:, 0, :].astype(F32)
    tiled = dot(bnd, (iota((border, ghosts), 1) % border == iota((border, ghosts), 0)).astype(F32))
    own_round = iota((rounds, ghosts), 1) // border == iota((rounds, ghosts), 0)
    brow = jnp.sum(jnp.where(own_round, tiled, 0.0), axis=0, keepdims=True).astype(jnp.int32)
    bt = (iota((nloc, ghosts), 0) == brow).astype(F32).astype(BF16)
    eye = (iota((nloc, nloc), 0) == iota((nloc, nloc), 1)).astype(F32).astype(BF16)
    b = dot_tn(bt, eye).astype(BF16)

    zero_w = jnp.zeros((chans, chans), BF16)
    w256[0] = jnp.concatenate(
        [
            jnp.concatenate([wr_ref[0], zero_w], axis=1),
            jnp.concatenate([zero_w, wr_ref[0]], axis=1),
        ],
        axis=0,
    )
    for m in range(1, LEVELS):
        w256[m] = jnp.concatenate(
            [
                jnp.concatenate([wr_ref[m], wi_ref[m - 1]], axis=1),
                jnp.concatenate([-wi_ref[m - 1], wr_ref[m]], axis=1),
            ],
            axis=0,
        )
    head_of = iota((chans, heads), 0) // width == iota((chans, heads), 1)
    gate_rows = dot(head_of.astype(F32), wg_ref[...].astype(F32)).astype(BF16)

    p0 = dot(nf[0], wr_ref[0])
    att = jax.nn.sigmoid(dot_nt(split(p0, 1), jnp.concatenate([gate_rows, gate_rows], axis=1)))
    att2 = jnp.concatenate([att, att], axis=1)
    q = jnp.concatenate([att * p0, jnp.zeros((nloc, chans), F32)], axis=1).astype(BF16)
    table[0, pl.ds(0, nloc), :] = q
    qout[0] = dot(b, q).astype(BF16)
    for chunk, orders in enumerate(CHUNK_ORDERS):
        for order in orders:
            n = pair_count(order)
            first = pair_comps(order, 0)[2]
            for i in range(n):
                ca, cb, slot = pair_comps(order, i)
                pairs[slot] = jnp.concatenate([nf[ca], nf[cb]], axis=1)
            p = dot(pairs[pl.ds(first, n)].reshape(n * nloc, 2 * chans), w256[order])
            p = p.reshape(n, nloc, 2 * chans)
            pbuf[pl.ds(first, n)] = p
            for i in range(n):
                q = (att2 * p[i]).astype(BF16)
                table[first + i, pl.ds(0, nloc), :] = q
                qout[first + i] = dot(b, q).astype(BF16)

    mine = pl.ds(pl.multiple_of(core * half, half), half)
    theirs = pl.ds(pl.multiple_of((1 - core) * half, half), half)

    def swap(batch):
        s = BATCHES.index(batch)
        at = pl.ds(*batch)
        return remote(xbuf.at[at, theirs, :], rcore.at[at], core_sem.at[s, 0], core_sem.at[s, 1], other)

    def scatter(batch, k):
        s = BATCHES.index(batch)
        at = pl.ds(*batch)
        own = pl.ds(pl.multiple_of(xy[k] * tile, tile), tile)
        return remote(part.at[at, own, :], rxy.at[k - 1, at], xs_sem.at[s], xr_sem.at[s], xy_device[k])

    def share(batch, k):
        s = BATCHES.index(batch)
        at = pl.ds(*batch)
        return remote(rz_own.at[at], rz.at[z_slot[k], at], zs_sem.at[s], zr_sem.at[s], z_device[k])

    def gather(batch, k):
        s = BATCHES.index(batch)
        ref = gathered[s].at[core, plane]
        return remote(ref, ref, gs_sem.at[s], gr_sem.at[s], xy_device[k])

    def swap_back(batch, core_half):
        s = BATCHES.index(batch)
        ref = gathered[s].at[core_half]
        return remote(ref, ref, core_sem.at[s, 2], core_sem.at[s, 3], other)

    def all_scatter(batch):
        s = BATCHES.index(batch)
        ref = rxy.at[:, pl.ds(*batch)]
        return remote(ref, ref, xs_sem.at[s], xr_sem.at[s], other)

    def all_share(batch):
        s = BATCHES.index(batch)
        ref = rz.at[pl.ds(0, 7), pl.ds(*batch)]
        return remote(ref, ref, zs_sem.at[s], zr_sem.at[s], other)

    def all_gather(batch):
        s = BATCHES.index(batch)
        ref = gathered[s].at[core, pl.ds(0, 15)]
        return remote(ref, ref, gs_sem.at[s], gr_sem.at[s], other)

    def after_swap(batch):
        swap(batch).wait_recv()
        at = pl.ds(*batch)
        part[at] = xbuf[at, mine, :] + rcore[at]
        for k in XY_FAR_FIRST:
            scatter(batch, k).start()

    def after_scatter(batch):
        at = pl.ds(*batch)
        total = part[at, pl.ds(pl.multiple_of(plane * tile, tile), tile), :]
        all_scatter(batch).wait_recv()
        for k in range(1, 16):
            total += rxy[k - 1, at]
        rz_own[at] = total
        for k in Z_FAR_FIRST:
            share(batch, k).start()

    def after_share(batch):
        at = pl.ds(*batch)
        all_share(batch).wait_recv()
        rz[zpos, at] = rz_own[at]
        total = rz[0, at]
        for k in range(1, 8):
            total += rz[k, at]
        total = total.reshape(batch[1] * tile, chans)
        ref = gathered[BATCHES.index(batch)]
        if ref.shape[2] > total.shape[0]:
            spare = jnp.zeros((ref.shape[2] - total.shape[0], chans), F32)
            total = jnp.concatenate([total, spare], axis=0)
        ref[core, plane] = total.astype(BF16)
        for k in XY_FAR_FIRST:
            gather(batch, k).start()

    def after_gather(batch):
        all_gather(batch).wait_recv()
        swap_back(batch, core).start()

    def unpack(batch):
        first, n = batch
        swap_back(batch, 1 - core).wait_recv()
        ref = gathered[BATCHES.index(batch)]
        for half_index in range(2):
            for j in range(16):
                t = ref[half_index, j].astype(F32)[: n * tile].reshape(n, tile, chans)
                full[pl.ds(first, n), pl.ds(half_index * half + j * tile, tile), :] = t

    def send_q(chunks, rounds_now):
        for chunk in chunks:
            for r in rounds_now:
                q_halo(chunk, r).start()

    v0 = None
    acc = None
    xbuf[0, pl.ds(chans, chans), :] = jnp.zeros((chans, chans), F32)
    for chunk, orders in enumerate(CHUNK_ORDERS):
        for r in range(rounds):
            v_halo(chunk, r).wait_recv()
        if chunk == 2:
            after_swap(E1)
        if chunk == 4:
            after_swap(E2)
        if chunk == 0:
            v0 = vown[0, :, pl.ds(0, chans)] + dot(bt, vin[0, :, pl.ds(0, chans)])
            acc = p0 * v0
        for order in orders:
            n = pair_count(order)
            first = pair_comps(order, 0)[2]
            z = []
            for i in range(n):
                v = vown[first + i] + dot(bt, vin[first + i])
                prod = pbuf[first + i] * v
                acc += prod[:, :chans] + prod[:, chans:]
                z.append(att2 * v)
            z = jnp.concatenate(z, axis=0)
            high = z.astype(BF16)
            low = (z - high.astype(F32)).astype(BF16)
            tc = dot_nt(high, w256[order]).reshape(n, nloc, 2 * chans)
            for i in range(n):
                ca, cb, slot = pair_comps(order, i)
                ng[ca] = cot[ca].astype(F32) + tc[i, :, :chans]
                ng[cb] = cot[cb].astype(F32) + tc[i, :, chans:]
            t = pairs[pl.ds(first, n)].reshape(n * nloc, 2 * chans)
            gw = dot_tn(jnp.concatenate([t, t], axis=0), jnp.concatenate([high, low], axis=0))
            real = gw[:chans, :chans] + gw[chans:, chans:]
            if order == 0:
                real += dot_tn(jnp.concatenate([nf[0], nf[0]], axis=0), split(att * v0, 0))
            else:
                xbuf[order, pl.ds(chans, chans), :] = gw[:chans, chans:] - gw[chans:, :chans]
            xbuf[order, pl.ds(0, chans), :] = real
        if chunk == 1:
            swap(E1).start()
        if chunk == 3:
            swap(E2).start()

    same_head = iota((chans, chans), 0) // width == iota((chans, chans), 1) // width
    same_head = same_head.astype(F32).astype(BF16)
    acc = dot(split(acc, 1), jnp.concatenate([same_head, same_head], axis=0))
    logit_cot = acc * att * (1.0 - att)
    lead = (iota((heads, chans), 1) == iota((heads, chans), 0) * width).astype(F32)
    outer = dot_tn(split(logit_cot, 0), jnp.concatenate([nf[0], nf[0]], axis=0))
    xbuf[0, pl.ds(chans, heads), :] = dot(lead, outer, HIGHEST)
    swap(LATE).start()

    def aggregate(q):
        u = dot(kt_mat, q)
        return u[:nloc] + u[nloc:]

    def forward(chunk):
        for r in range(rounds):
            q_halo(chunk, r).wait_recv()
        if chunk == 0:
            upd[0] = (nf[0].astype(F32) + aggregate(table[0, :, pl.ds(0, chans)])).astype(BF16)
        for order in CHUNK_ORDERS[chunk]:
            for i in range(pair_count(order)):
                ca, cb, slot = pair_comps(order, i)
                u = aggregate(table[slot])
                upd[ca] = (nf[ca].astype(F32) + u[:, :chans]).astype(BF16)
                upd[cb] = (nf[cb].astype(F32) + u[:, chans:]).astype(BF16)

    after_swap(LATE)
    send_q([0], [4, 3, 2, 1, 0])
    lead_rows = jnp.where(iota((chans, chans), 0) % width == 0, gate_rows.astype(F32), 0.0).astype(BF16)
    z0 = att * v0 + dot(split(logit_cot, 1), jnp.concatenate([lead_rows, lead_rows], axis=0))
    ng[0] = cot[0].astype(F32) + dot_nt(z0.astype(BF16), wr_ref[0])
    after_scatter(E1)
    after_scatter(E2)
    after_scatter(LATE)
    send_q([1, 2], [4, 3, 2, 1, 0])
    after_share(E1)
    after_share(E2)
    after_share(LATE)
    send_q([3, 4], [4, 3, 2, 1, 0])
    after_gather(E1)
    after_gather(E2)
    unpack(E1)
    unpack(E2)
    after_gather(LATE)
    forward(0)
    forward(1)
    forward(2)
    forward(3)
    forward(4)
    unpack(LATE)

    m_total = full[0, pl.ds(chans, heads), :]
    w0 = wr_ref[0]
    gate[...] = dot(split(m_total, 1), jnp.concatenate([w0, w0], axis=0))
    wg = wg_ref[...].astype(F32)
    late_real = dot_tn(split(m_total, 0), jnp.concatenate([wg, wg], axis=0).astype(BF16))
    real0[...] = full[0, pl.ds(0, chans), :] + late_real

    for chunk in range(len(CHUNKS)):
        for r in range(rounds):
            v_halo(chunk, r).wait_send()
            q_halo(chunk, r).wait_send()
    for batch in BATCHES:
        swap(batch).wait_send()
        all_scatter(batch).wait_send()
        all_share(batch).wait_send()
        all_gather(batch).wait_send()
        swap_back(batch, core).wait_send()


def store_kernel(upd, ng, full, real0, gate, upd_hbm, ng_hbm, real_hbm, imag_hbm, gate_hbm, sem):
    chans = real_hbm.shape[1]
    above = pl.ds(1, LEVELS - 1)
    copies = [
        (ng, ng_hbm),
        (upd, upd_hbm),
        (full.at[above, pl.ds(0, chans), :], real_hbm.at[above]),
        (full.at[above, pl.ds(chans, chans), :], imag_hbm),
        (real0, real_hbm.at[0]),
        (gate, gate_hbm),
    ]
    copies = [pltpu.make_async_copy(a, b, sem.at[i]) for i, (a, b) in enumerate(copies)]
    for copy in copies:
        copy.start()
    for copy in copies:
        copy.wait()


def shards(
    node_feats, cotangent, boundary, edge_src, edge_dst, edge_dist, edge_count, w_real, w_imag, w_gate
):
    nloc, comps, chans = node_feats.shape
    rounds, border = boundary.shape[1:]
    heads = w_gate.shape[1]
    ghosts = rounds * border
    rows = nloc + ghosts
    chunks = len(CHUNKS)
    pair = 2 * chans
    tile = chans // 16
    vmem = pl.BlockSpec(memory_space=pltpu.VMEM)
    hbm = pl.BlockSpec(memory_space=pltpu.HBM)
    dma = pltpu.SemaphoreType.DMA
    inputs = (
        node_feats.transpose(1, 0, 2),
        cotangent.transpose(1, 0, 2),
        boundary.transpose(1, 0, 2),
        edge_src,
        edge_dst,
        edge_dist,
        edge_count,
        w_real,
        w_imag,
        w_gate.T,
    )
    inputs = [
        a if a.ndim == 1 else pltpu.with_memory_space_constraint(a, pltpu.HBM) for a in inputs
    ]
    held = [
        (pltpu.SMEM if i == 6 else pltpu.VMEM)(a.shape, a.dtype) for i, a in enumerate(inputs)
    ]
    updated, node_grad, full, real0, gate = pl.pallas_call(
        main_kernel,
        out_shape=(
            pltpu.VMEM((comps, nloc, chans), BF16),
            pltpu.VMEM((comps, nloc, chans), F32),
            pltpu.VMEM((LEVELS, pair, chans), F32),
            pltpu.VMEM((chans, chans), F32),
            pltpu.VMEM((heads, chans), F32),
        ),
        in_specs=[hbm] * len(inputs),
        out_specs=(vmem,) * 5,
        scratch_shapes=held + [
            pltpu.VMEM((SLOTS, nloc, pair), BF16),
            pltpu.VMEM((SLOTS, ghosts, pair), BF16),
            pltpu.VMEM((SLOTS, ghosts, pair), BF16),
            pltpu.VMEM((SLOTS, nloc, pair), F32),
            pltpu.VMEM((SLOTS, ghosts, pair), BF16),
            pltpu.VMEM((SLOTS, rows, pair), BF16),
            pltpu.VMEM((SLOTS, nloc, pair), F32),
            pltpu.VMEM((LEVELS, pair, pair), BF16),
            pltpu.VMEM((LEVELS, pair, chans), F32),
            pltpu.VMEM((LEVELS, chans, chans), F32),
            pltpu.VMEM((LEVELS, chans, chans), F32),
            pltpu.VMEM((15, LEVELS, tile, chans), F32),
            pltpu.VMEM((LEVELS, tile, chans), F32),
            pltpu.VMEM((8, LEVELS, tile, chans), F32),
        ] + [
            pltpu.VMEM((2, 16, -(-n * tile // 16) * 16, chans), BF16) for _, n in BATCHES
        ] + [
            dma((len(inputs),)),
            dma((chunks, rounds)),
            dma((chunks, rounds)),
            dma((chunks, rounds)),
            dma((chunks, rounds)),
            dma((len(BATCHES), 4)),
            dma((len(BATCHES),)),
            dma((len(BATCHES),)),
            dma((len(BATCHES),)),
            dma((len(BATCHES),)),
            dma((len(BATCHES),)),
            dma((len(BATCHES),)),
        ],
        compiler_params=pltpu.CompilerParams(
            collective_id=0, has_side_effects=True, vmem_limit_bytes=40 * 2**20
        ),
        name="halo_edges",
    )(*inputs)
    updated, node_grad, real, imag, gate = pl.pallas_call(
        store_kernel,
        out_shape=(
            jax.ShapeDtypeStruct((comps, nloc, chans), BF16),
            jax.ShapeDtypeStruct((comps, nloc, chans), F32),
            jax.ShapeDtypeStruct((LEVELS, chans, chans), F32),
            jax.ShapeDtypeStruct((LEVELS - 1, chans, chans), F32),
            jax.ShapeDtypeStruct((heads, chans), F32),
        ),
        in_specs=[vmem] * 5,
        out_specs=(hbm,) * 5,
        scratch_shapes=[dma((6,))],
        compiler_params=pltpu.CompilerParams(vmem_limit_bytes=2 * 2**20),
        name="store",
    )(updated, node_grad, full, real0, gate)
    return (updated.transpose(1, 0, 2), node_grad.transpose(1, 0, 2), real, imag, gate.T)


def solution(mesh):
    whole = P("dom", None, None)
    return jax.shard_map(
        shards,
        mesh=mesh,
        in_specs=(
            whole, whole, whole, P("dom", None), P("dom", None), P("dom", None), P("dom"), P(), P(), P(),
        ),
        out_specs=(whole, whole, P(), P(), P()),
        check_vma=False,
    )
```

```python
import functools

import jax
import jax.numpy as jnp
from jax import lax
from jax.experimental import pallas as pl
from jax.experimental.pallas import tpu as pltpu
from jax.sharding import PartitionSpec as P

MESH = pl.DeviceIdType.MESH
F32 = jnp.float32
BF16 = jnp.bfloat16
HIGHEST = lax.Precision.HIGHEST

LEVELS = 7
SLOT0 = [0, 4, 10, 15, 19, 22, 24, 25]
SLOTS = 25
CHUNKS = [(0, 4), (19, 6), (15, 4), (10, 5), (4, 6)]
CHUNK_ORDERS = [[0], [4, 5, 6], [3], [2], [1]]
E1 = (4, 3)
E2 = (2, 2)
LATE = (0, 2)
BATCHES = [E1, E2, LATE]
XY_FAR_FIRST = sorted(range(1, 16), key=lambda k: -(min(k % 4, 4 - k % 4) + min(k // 4, 4 - k // 4)))
Z_FAR_FIRST = [4, 3, 5, 2, 6, 1, 7]


def dot(a, b, precision=None):
    return lax.dot_general(
        a, b, (((1,), (0,)), ((), ())), precision=precision, preferred_element_type=F32
    )


def dot_nt(a, b, precision=None):
    return lax.dot_general(
        a, b, (((1,), (1,)), ((), ())), precision=precision, preferred_element_type=F32
    )


def dot_tn(a, b, precision=None):
    return lax.dot_general(
        a, b, (((0,), (0,)), ((), ())), precision=precision, preferred_element_type=F32
    )


def iota(shape, dim):
    return lax.broadcasted_iota(jnp.int32, shape, dim)


def pair_comps(order, i):
    if order == 0:
        la = 2 * i + 1
        lb = 2 * i + 2
        return la * la + la, lb * lb + lb, 1 + i
    deg = i + order
    mid = deg * deg + deg
    return mid + order, mid - order, SLOT0[order] + i


def pair_count(order):
    return 3 if order == 0 else LEVELS - order


ALL_PAIRS = [(order, i) for order in range(LEVELS) for i in range(pair_count(order))]


def split(a, axis):
    high = a.astype(BF16)
    low = (a - high.astype(F32)).astype(BF16)
    return jnp.concatenate([high, low], axis=axis)


def remote(src, dst, send_sem, recv_sem, device):
    return pltpu.make_async_remote_copy(
        src_ref=src, dst_ref=dst, send_sem=send_sem, recv_sem=recv_sem,
        device_id=(device,), device_id_type=MESH,
    )


def main_kernel(
    nf_hbm, cot_hbm, bnd_hbm, src_hbm, dst_hbm, dist_hbm, cnt_hbm, wr_hbm, wi_hbm, wg_hbm,
    upd, ng, full, real0, gate,
    nf, cot, bnd_ref, src_ref, dst_ref, dist_ref, cnt_ref, wr_ref, wi_ref, wg_ref,
    pairs, vout, vin, vown, qout, table, pbuf, w256, xbuf, rcore, part, rxy, rz_own, rz, gathered0, gathered1, gathered2,
    in_sem, vs_sem, vr_sem, qs_sem, qr_sem, core_sem, xs_sem, xr_sem, zs_sem, zr_sem, gs_sem, gr_sem,
):
    gathered = [gathered0, gathered1, gathered2]
    rounds = bnd_ref.shape[0]
    border = bnd_ref.shape[2]
    nloc = nf.shape[1]
    ghosts = rounds * border
    rows = nloc + ghosts
    edges = src_ref.shape[1]
    chans = nf.shape[2]
    heads = wg_ref.shape[0]
    width = chans // heads
    me = lax.axis_index("dom")
    core = me % 2
    xpos = (me // 2) % 4
    zpos = (me // 8) % 8
    ypos = me // 64
    plane = ypos * 4 + xpos
    half = chans
    tile = half // 16
    partners = [me + (1 << r) * (1 - 2 * ((me // (1 << r)) % 2)) for r in range(rounds)]
    other = partners[0]
    xy = [((ypos + k // 4) % 4) * 4 + (xpos + k % 4) % 4 for k in range(16)]
    xy_device = [(j // 4) * 64 + zpos * 8 + (j % 4) * 2 + core for j in xy]
    z_from = [(zpos + 8 - k) % 8 for k in range(8)]
    z_slot = [zpos] * 8
    z_device = [ypos * 64 + ((zpos + k) % 8) * 8 + xpos * 2 + core for k in range(8)]

    sources = [cot_hbm, src_hbm, dst_hbm, dist_hbm, cnt_hbm, bnd_hbm, nf_hbm, wr_hbm, wi_hbm, wg_hbm]
    targets = [cot, src_ref, dst_ref, dist_ref, cnt_ref, bnd_ref, nf, wr_ref, wi_ref, wg_ref]
    loads = [
        pltpu.make_async_copy(a, b, in_sem.at[i]) for i, (a, b) in enumerate(zip(sources, targets))
    ]
    for load in loads:
        load.start()
    barrier = pltpu.get_barrier_semaphore()
    peers = [other] + xy_device[1:] + z_device[1:]
    for device in peers:
        pl.semaphore_signal(barrier, inc=1, device_id=(device,), device_id_type=MESH)

    for load in loads[1:5]:
        load.wait()
    live = (iota((1, edges), 1) < cnt_ref[0]).astype(F32)
    scale = (1.0 - dist_ref[...] / 5.0) ** 2 * live
    scaled = split(jnp.where(iota((rows, edges), 0) == src_ref[...], scale, 0.0), 0)
    into = (iota((nloc, edges), 0) == dst_ref[...]).astype(F32).astype(BF16)
    into2 = jnp.concatenate([into, into], axis=0)
    k2 = dot_nt(scaled, into2)
    k2 = 0.25 * (k2[:rows] + k2[rows:])
    high = k2.astype(BF16).astype(F32)
    k_mat = jnp.where(iota(k2.shape, 1) < nloc, high, k2 - high).astype(BF16)
    kt2 = dot_nt(into2, scaled[:rows]) + dot_nt(into2, scaled[rows:])
    kt2 = 0.25 * kt2
    high = kt2.astype(BF16).astype(F32)
    kt_mat = jnp.where(iota(kt2.shape, 0) < nloc, high, kt2 - high).astype(BF16)

    def v_halo(chunk, r):
        first, count = CHUNKS[chunk]
        at = (pl.ds(first, count), pl.ds(r * border, border), slice(None))
        return remote(vout.at[at], vin.at[at], vs_sem.at[chunk, r], vr_sem.at[chunk, r], partners[r])

    def q_halo(chunk, r):
        first, count = CHUNKS[chunk]
        return remote(
            qout.at[pl.ds(first, count), pl.ds(r * border, border), :],
            table.at[pl.ds(first, count), pl.ds(nloc + r * border, border), :],
            qs_sem.at[chunk, r], qr_sem.at[chunk, r], partners[r],
        )

    loads[0].wait()

    for chunk, orders in enumerate(CHUNK_ORDERS):
        if chunk == 0:
            v = dot(k_mat, jnp.concatenate([cot[0], cot[0]], axis=0))
            v = jnp.concatenate([v, jnp.zeros((rows, chans), F32)], axis=1)
            vown[0] = v[:nloc]
            vout[0] = v[nloc:].astype(BF16)
        for order in orders:
            for i in range(pair_count(order)):
                ca, cb, slot = pair_comps(order, i)
                both = jnp.concatenate([cot[ca], cot[cb]], axis=1)
                v = dot(k_mat, jnp.concatenate([both, both], axis=0))
                vown[slot] = v[:nloc]
                vout[slot] = v[nloc:].astype(BF16)
        if chunk == 0:
            pl.semaphore_wait(barrier, len(peers))
        for r in reversed(range(rounds)):
            v_halo(chunk, r).start()

    for load in loads[5:]:
        load.wait()
    bnd = bnd_ref[:, 0, :].astype(F32)
    tiled = dot(bnd, (iota((border, ghosts), 1) % border == iota((border, ghosts), 0)).astype(F32))
    own_round = iota((rounds, ghosts), 1) // border == iota((rounds, ghosts), 0)
    brow = jnp.sum(jnp.where(own_round, tiled, 0.0), axis=0, keepdims=True).astype(jnp.int32)
    bt = (iota((nloc, ghosts), 0) == brow).astype(F32).astype(BF16)
    eye = (iota((nloc, nloc), 0) == iota((nloc, nloc), 1)).astype(F32).astype(BF16)
    b = dot_tn(bt, eye).astype(BF16)

    zero_w = jnp.zeros((chans, chans), BF16)
    w256[0] = jnp.concatenate(
        [
            jnp.concatenate([wr_ref[0], zero_w], axis=1),
            jnp.concatenate([zero_w, wr_ref[0]], axis=1),
        ],
        axis=0,
    )
    for m in range(1, LEVELS):
        w256[m] = jnp.concatenate(
            [
                jnp.concatenate([wr_ref[m], wi_ref[m - 1]], axis=1),
                jnp.concatenate([-wi_ref[m - 1], wr_ref[m]], axis=1),
            ],
            axis=0,
        )
    head_of = iota((chans, heads), 0) // width == iota((chans, heads), 1)
    gate_rows = dot(head_of.astype(F32), wg_ref[...].astype(F32)).astype(BF16)

    p0 = dot(nf[0], wr_ref[0])
    att = jax.nn.sigmoid(dot_nt(split(p0, 1), jnp.concatenate([gate_rows, gate_rows], axis=1)))
    att2 = jnp.concatenate([att, att], axis=1)
    q = jnp.concatenate([att * p0, jnp.zeros((nloc, chans), F32)], axis=1).astype(BF16)
    table[0, pl.ds(0, nloc), :] = q
    qout[0] = dot(b, q).astype(BF16)
    for chunk, orders in enumerate(CHUNK_ORDERS):
        for order in orders:
            n = pair_count(order)
            first = pair_comps(order, 0)[2]
            for i in range(n):
                ca, cb, slot = pair_comps(order, i)
                pairs[slot] = jnp.concatenate([nf[ca], nf[cb]], axis=1)
            p = dot(pairs[pl.ds(first, n)].reshape(n * nloc, 2 * chans), w256[order])
            p = p.reshape(n, nloc, 2 * chans)
            pbuf[pl.ds(first, n)] = p
            for i in range(n):
                q = (att2 * p[i]).astype(BF16)
                table[first + i, pl.ds(0, nloc), :] = q
                qout[first + i] = dot(b, q).astype(BF16)

    mine = pl.ds(pl.multiple_of(core * half, half), half)
    theirs = pl.ds(pl.multiple_of((1 - core) * half, half), half)

    def swap(batch):
        s = BATCHES.index(batch)
        at = pl.ds(*batch)
        return remote(xbuf.at[at, theirs, :], rcore.at[at], core_sem.at[s, 0], core_sem.at[s, 1], other)

    def scatter(batch, k):
        s = BATCHES.index(batch)
        at = pl.ds(*batch)
        own = pl.ds(pl.multiple_of(xy[k] * tile, tile), tile)
        return remote(part.at[at, own, :], rxy.at[k - 1, at], xs_sem.at[s], xr_sem.at[s], xy_device[k])

    def share(batch, k):
        s = BATCHES.index(batch)
        at = pl.ds(*batch)
        return remote(rz_own.at[at], rz.at[z_slot[k], at], zs_sem.at[s], zr_sem.at[s], z_device[k])

    def gather(batch, k):
        s = BATCHES.index(batch)
        ref = gathered[s].at[core, plane]
        return remote(ref, ref, gs_sem.at[s], gr_sem.at[s], xy_device[k])

    def swap_back(batch, core_half):
        s = BATCHES.index(batch)
        ref = gathered[s].at[core_half]
        return remote(ref, ref, core_sem.at[s, 2], core_sem.at[s, 3], other)

    def all_scatter(batch):
        s = BATCHES.index(batch)
        ref = rxy.at[:, pl.ds(*batch)]
        return remote(ref, ref, xs_sem.at[s], xr_sem.at[s], other)

    def all_share(batch):
        s = BATCHES.index(batch)
        ref = rz.at[pl.ds(0, 7), pl.ds(*batch)]
        return remote(ref, ref, zs_sem.at[s], zr_sem.at[s], other)

    def all_gather(batch):
        s = BATCHES.index(batch)
        ref = gathered[s].at[core, pl.ds(0, 15)]
        return remote(ref, ref, gs_sem.at[s], gr_sem.at[s], other)

    def after_swap(batch):
        swap(batch).wait_recv()
        at = pl.ds(*batch)
        part[at] = xbuf[at, mine, :] + rcore[at]
        for k in XY_FAR_FIRST:
            scatter(batch, k).start()

    def after_scatter(batch):
        at = pl.ds(*batch)
        total = part[at, pl.ds(pl.multiple_of(plane * tile, tile), tile), :]
        all_scatter(batch).wait_recv()
        for k in range(1, 16):
            total += rxy[k - 1, at]
        rz_own[at] = total
        for k in Z_FAR_FIRST:
            share(batch, k).start()

    def after_share(batch):
        at = pl.ds(*batch)
        all_share(batch).wait_recv()
        rz[zpos, at] = rz_own[at]
        total = rz[0, at]
        for k in range(1, 8):
            total += rz[k, at]
        total = total.reshape(batch[1] * tile, chans)
        ref = gathered[BATCHES.index(batch)]
        if ref.shape[2] > total.shape[0]:
            spare = jnp.zeros((ref.shape[2] - total.shape[0], chans), F32)
            total = jnp.concatenate([total, spare], axis=0)
        ref[core, plane] = total.astype(BF16)
        for k in XY_FAR_FIRST:
            gather(batch, k).start()

    def after_gather(batch):
        all_gather(batch).wait_recv()
        swap_back(batch, core).start()

    def unpack(batch):
        first, n = batch
        swap_back(batch, 1 - core).wait_recv()
        ref = gathered[BATCHES.index(batch)]
        for half_index in range(2):
            for j in range(16):
                t = ref[half_index, j].astype(F32)[: n * tile].reshape(n, tile, chans)
                full[pl.ds(first, n), pl.ds(half_index * half + j * tile, tile), :] = t

    def send_q(chunks, rounds_now):
        for chunk in chunks:
            for r in rounds_now:
                q_halo(chunk, r).start()

    v0 = None
    acc = None
    xbuf[0, pl.ds(chans, chans), :] = jnp.zeros((chans, chans), F32)
    for chunk, orders in enumerate(CHUNK_ORDERS):
        for r in range(rounds):
            v_halo(chunk, r).wait_recv()
        if chunk == 2:
            after_swap(E1)
        if chunk == 4:
            after_swap(E2)
        if chunk == 0:
            v0 = vown[0, :, pl.ds(0, chans)] + dot(bt, vin[0, :, pl.ds(0, chans)])
            acc = p0 * v0
        for order in orders:
            n = pair_count(order)
            first = pair_comps(order, 0)[2]
            z = []
            for i in range(n):
                v = vown[first + i] + dot(bt, vin[first + i])
                prod = pbuf[first + i] * v
                acc += prod[:, :chans] + prod[:, chans:]
                z.append(att2 * v)
            z = jnp.concatenate(z, axis=0)
            high = z.astype(BF16)
            low = (z - high.astype(F32)).astype(BF16)
            tc = dot_nt(high, w256[order]).reshape(n, nloc, 2 * chans)
            for i in range(n):
                ca, cb, slot = pair_comps(order, i)
                ng[ca] = cot[ca].astype(F32) + tc[i, :, :chans]
                ng[cb] = cot[cb].astype(F32) + tc[i, :, chans:]
            t = pairs[pl.ds(first, n)].reshape(n * nloc, 2 * chans)
            gw = dot_tn(jnp.concatenate([t, t], axis=0), jnp.concatenate([high, low], axis=0))
            real = gw[:chans, :chans] + gw[chans:, chans:]
            if order == 0:
                real += dot_tn(jnp.concatenate([nf[0], nf[0]], axis=0), split(att * v0, 0))
            else:
                xbuf[order, pl.ds(chans, chans), :] = gw[:chans, chans:] - gw[chans:, :chans]
            xbuf[order, pl.ds(0, chans), :] = real
        if chunk == 1:
            swap(E1).start()
        if chunk == 3:
            swap(E2).start()

    same_head = iota((chans, chans), 0) // width == iota((chans, chans), 1) // width
    same_head = same_head.astype(F32).astype(BF16)
    acc = dot(split(acc, 1), jnp.concatenate([same_head, same_head], axis=0))
    logit_cot = acc * att * (1.0 - att)
    outer = dot_tn(split(logit_cot, 0), jnp.concatenate([nf[0], nf[0]], axis=0))
    xbuf[0, pl.ds(chans, heads), :] = outer.reshape(heads, width, chans)[:, 0, :]
    swap(LATE).start()

    def aggregate(q):
        u = dot(kt_mat, q)
        return u[:nloc] + u[nloc:]

    def forward(chunk):
        for r in range(rounds):
            q_halo(chunk, r).wait_recv()
        if chunk == 0:
            upd[0] = (nf[0].astype(F32) + aggregate(table[0, :, pl.ds(0, chans)])).astype(BF16)
        for order in CHUNK_ORDERS[chunk]:
            for i in range(pair_count(order)):
                ca, cb, slot = pair_comps(order, i)
                u = aggregate(table[slot])
                upd[ca] = (nf[ca].astype(F32) + u[:, :chans]).astype(BF16)
                upd[cb] = (nf[cb].astype(F32) + u[:, chans:]).astype(BF16)

    after_swap(LATE)
    send_q([0], [4, 3, 2, 1, 0])
    lead_rows = jnp.where(iota((chans, chans), 0) % width == 0, gate_rows.astype(F32), 0.0).astype(BF16)
    z0 = att * v0 + dot(split(logit_cot, 1), jnp.concatenate([lead_rows, lead_rows], axis=0))
    ng[0] = cot[0].astype(F32) + dot_nt(z0.astype(BF16), wr_ref[0])
    after_scatter(E1)
    after_scatter(E2)
    after_scatter(LATE)
    send_q([1, 2], [4, 3, 2, 1, 0])
    after_share(E1)
    after_share(E2)
    after_share(LATE)
    send_q([3, 4], [4, 3, 2, 1, 0])
    after_gather(E1)
    after_gather(E2)
    unpack(E1)
    unpack(E2)
    after_gather(LATE)
    forward(0)
    forward(1)
    forward(2)
    forward(3)
    forward(4)
    unpack(LATE)

    m_total = full[0, pl.ds(chans, heads), :]
    w0 = wr_ref[0]
    gate[...] = dot(split(m_total, 1), jnp.concatenate([w0, w0], axis=0))
    wg = wg_ref[...].astype(F32)
    late_real = dot_tn(split(m_total, 0), jnp.concatenate([wg, wg], axis=0).astype(BF16))
    real0[...] = full[0, pl.ds(0, chans), :] + late_real

    for chunk in range(len(CHUNKS)):
        for r in range(rounds):
            v_halo(chunk, r).wait_send()
            q_halo(chunk, r).wait_send()
    for batch in BATCHES:
        swap(batch).wait_send()
        all_scatter(batch).wait_send()
        all_share(batch).wait_send()
        all_gather(batch).wait_send()
        swap_back(batch, core).wait_send()


def store_kernel(upd, ng, full, real0, gate, upd_hbm, ng_hbm, real_hbm, imag_hbm, gate_hbm, sem):
    chans = real_hbm.shape[1]
    above = pl.ds(1, LEVELS - 1)
    copies = [
        (ng, ng_hbm),
        (upd, upd_hbm),
        (full.at[above, pl.ds(0, chans), :], real_hbm.at[above]),
        (full.at[above, pl.ds(chans, chans), :], imag_hbm),
        (real0, real_hbm.at[0]),
        (gate, gate_hbm),
    ]
    copies = [pltpu.make_async_copy(a, b, sem.at[i]) for i, (a, b) in enumerate(copies)]
    for copy in copies:
        copy.start()
    for copy in copies:
        copy.wait()


def shards(
    node_feats, cotangent, boundary, edge_src, edge_dst, edge_dist, edge_count, w_real, w_imag, w_gate
):
    nloc, comps, chans = node_feats.shape
    rounds, border = boundary.shape[1:]
    heads = w_gate.shape[1]
    ghosts = rounds * border
    rows = nloc + ghosts
    chunks = len(CHUNKS)
    pair = 2 * chans
    tile = chans // 16
    vmem = pl.BlockSpec(memory_space=pltpu.VMEM)
    hbm = pl.BlockSpec(memory_space=pltpu.HBM)
    dma = pltpu.SemaphoreType.DMA
    inputs = (
        node_feats.transpose(1, 0, 2),
        cotangent.transpose(1, 0, 2),
        boundary.transpose(1, 0, 2),
        edge_src,
        edge_dst,
        edge_dist,
        edge_count,
        w_real,
        w_imag,
        w_gate.T,
    )
    inputs = [
        a if a.ndim == 1 else pltpu.with_memory_space_constraint(a, pltpu.HBM) for a in inputs
    ]
    held = [
        (pltpu.SMEM if i == 6 else pltpu.VMEM)(a.shape, a.dtype) for i, a in enumerate(inputs)
    ]
    updated, node_grad, full, real0, gate = pl.pallas_call(
        main_kernel,
        out_shape=(
            pltpu.VMEM((comps, nloc, chans), BF16),
            pltpu.VMEM((comps, nloc, chans), F32),
            pltpu.VMEM((LEVELS, pair, chans), F32),
            pltpu.VMEM((chans, chans), F32),
            pltpu.VMEM((heads, chans), F32),
        ),
        in_specs=[hbm] * len(inputs),
        out_specs=(vmem,) * 5,
        scratch_shapes=held + [
            pltpu.VMEM((SLOTS, nloc, pair), BF16),
            pltpu.VMEM((SLOTS, ghosts, pair), BF16),
            pltpu.VMEM((SLOTS, ghosts, pair), BF16),
            pltpu.VMEM((SLOTS, nloc, pair), F32),
            pltpu.VMEM((SLOTS, ghosts, pair), BF16),
            pltpu.VMEM((SLOTS, rows, pair), BF16),
            pltpu.VMEM((SLOTS, nloc, pair), F32),
            pltpu.VMEM((LEVELS, pair, pair), BF16),
            pltpu.VMEM((LEVELS, pair, chans), F32),
            pltpu.VMEM((LEVELS, chans, chans), F32),
            pltpu.VMEM((LEVELS, chans, chans), F32),
            pltpu.VMEM((15, LEVELS, tile, chans), F32),
            pltpu.VMEM((LEVELS, tile, chans), F32),
            pltpu.VMEM((8, LEVELS, tile, chans), F32),
        ] + [
            pltpu.VMEM((2, 16, -(-n * tile // 16) * 16, chans), BF16) for _, n in BATCHES
        ] + [
            dma((len(inputs),)),
            dma((chunks, rounds)),
            dma((chunks, rounds)),
            dma((chunks, rounds)),
            dma((chunks, rounds)),
            dma((len(BATCHES), 4)),
            dma((len(BATCHES),)),
            dma((len(BATCHES),)),
            dma((len(BATCHES),)),
            dma((len(BATCHES),)),
            dma((len(BATCHES),)),
            dma((len(BATCHES),)),
        ],
        compiler_params=pltpu.CompilerParams(
            collective_id=0, has_side_effects=True, vmem_limit_bytes=40 * 2**20
        ),
        name="halo_edges",
    )(*inputs)
    updated, node_grad, real, imag, gate = pl.pallas_call(
        store_kernel,
        out_shape=(
            jax.ShapeDtypeStruct((comps, nloc, chans), BF16),
            jax.ShapeDtypeStruct((comps, nloc, chans), F32),
            jax.ShapeDtypeStruct((LEVELS, chans, chans), F32),
            jax.ShapeDtypeStruct((LEVELS - 1, chans, chans), F32),
            jax.ShapeDtypeStruct((heads, chans), F32),
        ),
        in_specs=[vmem] * 5,
        out_specs=(hbm,) * 5,
        scratch_shapes=[dma((6,))],
        compiler_params=pltpu.CompilerParams(vmem_limit_bytes=2 * 2**20),
        name="store",
    )(updated, node_grad, full, real0, gate)
    return (updated.transpose(1, 0, 2), node_grad.transpose(1, 0, 2), real, imag, gate.T)


def solution(mesh):
    whole = P("dom", None, None)
    return jax.shard_map(
        shards,
        mesh=mesh,
        in_specs=(
            whole, whole, whole, P("dom", None), P("dom", None), P("dom", None), P("dom"), P(), P(), P(),
        ),
        out_specs=(whole, whole, P(), P(), P()),
        check_vma=False,
    )
```
